768 devices in a mesh: feat: 12 (over z), dom: 64 (over y, x, core).
Axes of the slice: x: 4, y: 8, z: 12, core: 2. Of those that a mesh axis runs over, the one named last changes fastest.
Arguments:
- features: bfloat16 [64, 1536, 768], P('dom', None, 'feat'), may hold values from -6 to 6
- tiles: bfloat16 [64, 36, 128, 128], P('dom')
- tile_ids: int32 [64, 36, 2], P('dom'), may hold values from 0 to 11, as said below
- sources: int32 [64, 64, 12, 16], P('dom'), may hold values from 0 to 1535
- targets: int32 [64, 64, 12, 16], P('dom'), may hold values from 0 to 127
- counts: int32 [64, 64, 12], P('dom'), may hold values from 0 to 16, as said below
- edge_weight: bfloat16 [64, 64, 12, 16], P('dom'), may hold values from 0.5 to 2
- self_one: bfloat16 [768, 1024], replicated, may hold values from -0.21875 to 0.21875
- neigh_one: bfloat16 [768, 1024], replicated, may hold values from -0.21875 to 0.21875
- self_out: bfloat16 [1024, 153], replicated, may hold values from -0.1875 to 0.1875
- neigh_out: bfloat16 [1024, 153], replicated, may hold values from -0.1875 to 0.1875
Outputs:
- hidden: bfloat16 [64, 1536, 1024], P('dom', 'feat')
- logits: float32 [64, 153, 1536], P('dom', None, 'feat')
The draws below stay inside these ranges and needn't reach their ends.
Inputs may be any that keep to these rules, and one draw needn't show every extreme that they name: `tile_ids`: in each partition the 36 (row block, column block) pairs are distinct, and every row block appears in exactly 3 of them, in no fixed order. counts[e, e, g] is 0; in every draw some partition receives 16 live slots from every other partition in every group.
All inputs are finite; a program needn't handle non-finite values.
Results may differ from the reference program's by a relative error of at most 0.003.
Values may be sent and summed in bfloat16 or wider, within the bound.
A program may use at most 64 MiB of HBM per device.

```python
import math
import jax
import jax.numpy as jnp
from jax import lax

F = 768
HID = 1024
CLASSES = 153
TILE = 128
NODE_BLKS = 1
TILE_ROW = 3
SLOTS = 16
ROWS = 128
PART_NODES = 1536
N_FEAT = 12
N_DOM = 64


def draw_tiles(key, part):
    key = jax.random.fold_in(key, 5)
    shape = (N_DOM, TILE_ROW * NODE_BLKS * N_FEAT, TILE, TILE)
    uniform_values = jax.random.uniform(key, shape, jnp.float32)
    entry_values = uniform_values * (2.0 / TILE)
    return entry_values.astype(jnp.bfloat16)


def draw_tile_ids(key, part):
    key = jax.random.fold_in(key, 11)
    key_cols, key_order = jax.random.split(key)
    block_count = NODE_BLKS * N_FEAT
    tile_total = block_count * TILE_ROW
    scores = jax.random.randint(key_cols, (N_DOM, block_count, block_count), 0, 1 << 20)
    scores = scores * block_count + jnp.arange(block_count, dtype=jnp.int32)
    ranked = jnp.argsort(scores, axis=2, stable=True)[:, :, :TILE_ROW].astype(jnp.int32)
    row_ids = jnp.broadcast_to(jnp.arange(block_count, dtype=jnp.int32)[None, :, None], ranked.shape)
    listed = jnp.stack([row_ids, ranked], axis=-1).reshape(N_DOM, tile_total, 2)
    order_scores = jax.random.randint(key_order, (N_DOM, tile_total), 0, 1 << 20) * tile_total
    order_scores = order_scores + jnp.arange(tile_total, dtype=jnp.int32)
    order = jnp.argsort(order_scores, axis=1, stable=True)
    return jnp.take_along_axis(listed, order[:, :, None], axis=1).astype(jnp.int32)


def draw_counts(key, part):
    key = jax.random.fold_in(key, 23)
    key_base, key_crowd, key_pick = jax.random.split(key, 3)
    drawn = jax.random.randint(key_base, (N_DOM, N_DOM, N_FEAT), 0, SLOTS + 1)
    crowded = jax.random.randint(key_crowd, (N_DOM,), 0, 4) == 0
    chosen_one = jax.random.randint(key_pick, (), 0, N_DOM)
    crowded = crowded | (jnp.arange(N_DOM) == chosen_one)
    filled = jnp.where(crowded[:, None, None], SLOTS, drawn)
    diagonal = jnp.arange(N_DOM)[:, None] == jnp.arange(N_DOM)[None, :]
    return jnp.where(diagonal[:, :, None], 0, filled).astype(jnp.int32)


def plant(values, stream_key, smallest, high):
    spot = [jax.random.randint(jax.random.fold_in(stream_key, axis), (), 0, length) for axis, length in enumerate(values.shape)]
    widest = values.shape.index(max(values.shape))
    neighbour = spot[:widest] + [(spot[widest] + 1) % values.shape[widest]] + spot[widest + 1:]
    return values.at[tuple(spot)].set(smallest).at[tuple(neighbour)].set(high)


def shard_levels(own_key, extent, pieces, smallest, largest):
    loudness, own = 1.0, jax.random.fold_in(own_key, 6)
    for dim, blocks in pieces:
        steps = jnp.exp(jax.random.uniform(jax.random.fold_in(own, dim), (blocks,), jnp.float32, smallest / len(pieces), largest / len(pieces)))
        loudness = loudness * jnp.repeat(steps, extent[dim] // blocks).reshape([-1 if axis == dim else 1 for axis in range(len(extent))])
    return loudness


def bell_draw(rng, extent, deviation, bound, cuts=(), kind=jnp.bfloat16):
    array = deviation * jax.random.normal(rng, extent, jnp.float32)
    if cuts:
        array = array * shard_levels(rng, extent, cuts, -0.22, 0.18)
    return jnp.clip(array, -bound, bound).astype(kind)


def setup_inputs(seed: int = 0) -> dict:
    seeds = jax.random.split(jax.random.key(seed), 12)
    features = bell_draw(seeds[0], (N_DOM, PART_NODES, F), 1.0, 6.0, ((0, 64), (2, 12)))
    tiles = draw_tiles(jax.random.fold_in(seeds[11], 71), 0)
    tile_ids = draw_tile_ids(jax.random.fold_in(seeds[11], 71), 0)
    sources = plant(jax.random.randint(seeds[3], (N_DOM, N_DOM, N_FEAT, SLOTS), 0, PART_NODES), jax.random.fold_in(seeds[3], 1), 0, PART_NODES - 1).astype(jnp.int32)
    targets = plant(jax.random.randint(seeds[4], (N_DOM, N_DOM, N_FEAT, SLOTS), 0, ROWS), jax.random.fold_in(seeds[4], 1), 0, ROWS - 1).astype(jnp.int32)
    counts = draw_counts(jax.random.fold_in(seeds[11], 71), 0)
    edge_weight = jnp.clip(jnp.exp(math.log(2.0) - 1.3862944 * jax.random.uniform(seeds[6], (N_DOM, N_DOM, N_FEAT, SLOTS), jnp.float32) ** shard_levels(seeds[6], (N_DOM, N_DOM, N_FEAT, SLOTS), ((0, 64),), -0.2, 0.2)), 0.5, 2.0).astype(jnp.bfloat16)
    self_one = bell_draw(seeds[7], (F, HID), F ** -0.5, 0.21875)
    neigh_one = bell_draw(seeds[8], (F, HID), F ** -0.5, 0.21875)
    self_out = bell_draw(seeds[9], (HID, CLASSES), HID ** -0.5, 0.1875)
    neigh_out = bell_draw(seeds[10], (HID, CLASSES), HID ** -0.5, 0.1875)
    return {"features": features, "tiles": tiles, "tile_ids": tile_ids, "sources": sources, "targets": targets, "counts": counts, "edge_weight": edge_weight, "self_one": self_one, "neigh_one": neigh_one, "self_out": self_out, "neigh_out": neigh_out}


def block_sum(tile_contents, tile_pairs, feature_field_rows):
    block_count = feature_field_rows.shape[0] // TILE
    blocks = feature_field_rows.reshape(block_count, TILE, feature_field_rows.shape[1]).astype(jnp.float32)
    picked = jnp.take(blocks, tile_pairs[:, 1], axis=0)
    products = jnp.einsum("tij,tjc->tic", tile_contents.astype(jnp.float32), picked, precision=lax.Precision.HIGHEST)
    owners = (tile_pairs[:, 0][:, None] == jnp.arange(block_count, dtype=jnp.int32)[None, :]).astype(jnp.float32)
    summed = jnp.einsum("tb,tic->bic", owners, products, precision=lax.Precision.HIGHEST)
    return summed.reshape(feature_field_rows.shape[0], feature_field_rows.shape[1])


def edge_matrix(target_part, count_part, weight_part):
    slot_live = jnp.arange(SLOTS, dtype=jnp.int32)[None, None, :] < count_part[:, :, None]
    kept_weights = jnp.where(slot_live, weight_part.astype(jnp.float32), 0.0)
    target_hits = (target_part[..., None] == jnp.arange(ROWS, dtype=jnp.int32)).astype(jnp.float32)
    return target_hits * kept_weights[..., None]


def reference(features, tiles, tile_ids, sources, targets, counts, edge_weight, self_one, neigh_one, self_out, neigh_out):
    partitions = jnp.arange(N_DOM, dtype=jnp.int32)

    def edge_parts(partition):
        edge_matrices = edge_matrix(targets[partition], counts[partition], edge_weight[partition])
        ones_field = jnp.ones((PART_NODES, 1), jnp.float32)
        tile_degree = block_sum(tiles[partition], tile_ids[partition], ones_field)[:, 0]
        degree = tile_degree + jnp.sum(edge_matrices, axis=(0, 2)).reshape(PART_NODES)
        return edge_matrices, degree

    def boundary_term(edge_matrices, field_all, partition):
        picks = sources[:, partition]
        entry_values = field_all[partitions[:, None, None], picks].astype(jnp.float32)
        summed = jnp.einsum("dgsr,dgsc->grc", edge_matrices, entry_values, precision=lax.Precision.HIGHEST)
        return summed.reshape(PART_NODES, field_all.shape[2])

    def first_layer(partition):
        edge_matrices, degree = edge_parts(partition)
        own_rows = features[partition]
        edge_term = boundary_term(edge_matrices, features, partition)
        local_term = block_sum(tiles[partition], tile_ids[partition], own_rows)
        neighbours = ((local_term + edge_term) / degree[:, None]).astype(jnp.bfloat16)
        preact = jnp.dot(own_rows, self_one, preferred_element_type=jnp.float32) + jnp.dot(neighbours, neigh_one, preferred_element_type=jnp.float32)
        return jnp.maximum(preact, 0.0).astype(jnp.bfloat16)

    hidden = lax.map(first_layer, partitions)

    def last_layer(partition):
        edge_matrices, degree = edge_parts(partition)
        own_rows = hidden[partition]
        edge_term = boundary_term(edge_matrices, hidden, partition)
        local_term = block_sum(tiles[partition], tile_ids[partition], own_rows)
        mean_two = (local_term + edge_term) / degree[:, None]
        scores = jnp.dot(own_rows, self_out, preferred_element_type=jnp.float32)
        scores = scores + jnp.dot(mean_two, neigh_out.astype(jnp.float32), precision=lax.Precision.HIGHEST)
        return scores.T

    logits = lax.map(last_layer, partitions)
    return hidden, logits
```

```python
import jax
import jax.numpy as jnp
from jax import lax
from jax.experimental import pallas as pl
from jax.experimental.pallas import tpu as pltpu
from jax.sharding import PartitionSpec as P

MESH = pl.DeviceIdType.MESH
BF = jnp.bfloat16
F32 = jnp.float32
I32 = jnp.int32
NT = (((1,), (1,)), ((), ()))

NF = 12
ND = 64
NY = 8
NX = 8
COLS = 64
NODES = 1536
HID = 1024
CLS = 153
CPAD = 160
PAIRS = ((0, 1), (2, 7), (6, 3), (4, 5))


def iota(shape, dim):
    return lax.broadcasted_iota(I32, shape, dim)


def mod(a, n):
    return lax.rem(a, jnp.int32(n))


def dot(a, b):
    return jnp.dot(a, b, preferred_element_type=F32)


def dot_nt(a, b):
    return lax.dot_general(a, b, NT, preferred_element_type=F32)


def kernel(
    ids, counts, sources, targets, weights, feat, tiles_hbm, s1_hbm, n1_hbm, so, no,
    hidden_ref, logits_ref,
    tiles, s1, n1, tab, idx_out, idx_in, picked, out1, in1, ftd, scat, rows_t, rows_w, acc,
    frows, nsend_buf, nrows, pre, wso, wno, z, oh2, scat2, out2, in2, deg, prod, band,
    loc, tsend, trecv, isend, irecv, fsend, frecv, xsend, xrecv, nsend, nrecv, zsend, zrecv, asend, arecv,
):
    f = lax.axis_index("feat")
    d = lax.axis_index("dom")
    y = lax.div(d, jnp.int32(NX))
    xc = mod(d, NX)
    core = mod(d, 2)

    loads = [
        pltpu.make_async_copy(tiles_hbm, tiles, loc.at[0]),
        pltpu.make_async_copy(s1_hbm, s1, loc.at[1]),
        pltpu.make_async_copy(n1_hbm, n1, loc.at[2]),
    ]
    for load in loads:
        load.start()

    def remote(src, dst, ss, rs, fi, di):
        return pltpu.make_async_remote_copy(
            src_ref=src, dst_ref=dst, send_sem=ss, recv_sem=rs, device_id=(fi, di), device_id_type=MESH
        )

    def arrived(dst, rs):
        pltpu.make_async_copy(dst, dst, rs).wait()

    def row_peer(k):
        return mod(y + k, NY) * NX + xc

    def col_peer(k):
        return y * NX + mod(xc + k, NX)

    barrier = pltpu.get_barrier_semaphore()
    for k in range(1, NY):
        pl.semaphore_signal(barrier, inc=1, device_id=(f, row_peer(k)), device_id_type=MESH)
    for k in range(1, NX):
        pl.semaphore_signal(barrier, inc=1, device_id=(f, col_peer(k)), device_id_type=MESH)
    for k in range(1, NF):
        pl.semaphore_signal(barrier, inc=1, device_id=(mod(f + k, NF), d), device_id_type=MESH)

    src = sources[...].reshape(192, ND)
    both = jnp.concatenate([src >> 8, src & 255], axis=0).astype(F32).astype(BF)
    r32 = iota((32, ND), 0)
    e32 = iota((32, ND), 1)
    flip = (lax.div(r32, 4) + y) & 1
    halves = []
    for h in range(2):
        pick = (e32 == r32 * 2 + (flip ^ h)).astype(F32).astype(BF)
        got = dot_nt(pick, both)
        halves.append((got[:, :192] * 256.0 + got[:, 192:]).astype(I32))
    for q in range(3):
        tile = jnp.concatenate([halves[0][:, q * 64 : q * 64 + 64], halves[1][:, q * 64 : q * 64 + 64]], axis=1)
        for row in range(NY):
            idx_out[row, q * 4 : q * 4 + 4, :] = tile[row * 4 : row * 4 + 4]
    idx_in[0] = idx_out[y]

    pl.semaphore_wait(barrier, NY - 1 + NX - 1 + NF - 1)

    sent = []

    def go(copy):
        copy.start()
        sent.append(copy)

    def table(slot):
        return feat if slot == 0 else tab.at[slot]

    def pass_on(from_slot, to_slot, half, di):
        part = pl.ds(half * 768, 768)
        go(remote(
            table(from_slot).at[:, part], tab.at[to_slot, :, part],
            tsend.at[to_slot, half], trecv.at[to_slot, half], f, di,
        ))

    def took(slot, half):
        arrived(tab.at[slot, :, pl.ds(half * 768, 768)], trecv.at[slot, half])

    up = row_peer(1)
    down = row_peer(NY - 1)
    for half in range(2):
        pass_on(0, 1, half, up)
        pass_on(0, 7, half, down)
    for k in range(1, NY):
        to = mod(y + k, NY)
        go(remote(idx_out.at[to], idx_in.at[k], isend.at[k], irecv.at[k], f, to * NX + xc))
    for k in range(1, NF):
        g = mod(f + k, NF)
        go(remote(
            feat.at[:, pl.ds(pl.multiple_of(g * 128, 128), 128)], frows.at[f], fsend.at[k], frecv.at[k], g, d
        ))
    frows[f] = feat[:, pl.ds(pl.multiple_of(f * 128, 128), 128)]

    def gather(slot):
        @pl.loop(0, 6)
        def _(r):
            here = table(slot)
            wide = jnp.concatenate([here[:, k * 256 : k * 256 + 256] for k in range(6)], axis=0)
            pick = jnp.concatenate(
                [idx_in[slot, pl.ds(2 * r, 1), :], idx_in[slot, pl.ds(2 * r + 1, 1), :]], axis=1
            )
            low = pick & 255
            high = pick >> 8
            one_hot = (iota((256, 256), 0) == low).astype(F32).astype(BF)
            got = dot(wide, one_hot)
            kept = jnp.zeros((COLS, 256), F32)
            for k in range(6):
                kept = jnp.where(high == k, got[k * COLS : k * COLS + COLS], kept)
            picked[slot, :, pl.ds(pl.multiple_of(r * 256, 256), 256)] = kept.astype(BF)

    first_half = iota((COLS, 128), 1) < 64

    def merge_and_send(b):
        even, odd = PAIRS[b]
        for q in range(3):
            for col in range(4):
                at = (q * 4 + col) * 128
                one = picked[even, :, at : at + 128]
                two = picked[odd, :, at : at + 128]
                out1[b, 2 * col, :, q * 128 : q * 128 + 128] = jnp.where(first_half, one, two)
                out1[b, 2 * col + 1, :, q * 128 : q * 128 + 128] = jnp.where(first_half, two, one)
        for k in (4, 3, 5, 2, 6, 1, 7):
            to = mod(xc + k, NX)
            go(remote(
                out1.at[b, to], in1.at[b, xc, pl.ds(0, COLS)], xsend.at[b, k], xrecv.at[b, k], f, y * NX + to
            ))
        in1[b, xc, 0:COLS] = out1[b, xc]

    gather(0)

    live = iota((NF, 16, ND), 1) < counts[...]
    t_all = jnp.where(live, targets[...], -512).reshape(192, ND)
    w_all = weights[...].reshape(192, ND)
    both = jnp.concatenate([t_all.astype(F32).astype(BF), w_all], axis=0)
    batch = lax.div(r32, 8)
    halves = []
    for h in range(2):
        par = core ^ h
        far = jnp.zeros((32, ND), I32)
        for b in range(4):
            dist = jnp.where(par == 0, PAIRS[b][0], PAIRS[b][1])
            far = jnp.where(batch == b, dist, far)
        origin = ((y + 8 - far) & 7) * 8 + (r32 & 7)
        halves.append(dot_nt((e32 == origin).astype(F32).astype(BF), both))
    for q in range(3):
        lanes = iota((32, 128), 1)
        base = (lax.div(lanes, 16) & 3) * 128
        t_tile = jnp.concatenate([halves[0][:, q * 64 : q * 64 + 64], halves[1][:, q * 64 : q * 64 + 64]], axis=1)
        w_tile = jnp.concatenate(
            [halves[0][:, 192 + q * 64 : 256 + q * 64], halves[1][:, 192 + q * 64 : 256 + q * 64]], axis=1
        )
        rows_t[q] = t_tile.astype(I32) + base
        rows_w[q] = w_tile

    def build(b):
        @pl.loop(0, 8)
        def _(i):
            r = b * 8 + i
            for q in range(3):
                t = rows_t[q, pl.ds(r, 1), :]
                w = rows_w[q, pl.ds(r, 1), :]
                scat[q, :, pl.ds(pl.multiple_of(r * 128, 128), 128)] = jnp.where(
                    iota((512, 128), 0) == t, w, 0.0
                ).astype(BF)

    def scatter(b):
        for k in range(1, NX):
            arrived(in1.at[b, mod(xc + NX - k, NX), pl.ds(0, COLS)], xrecv.at[b, k])
        for q in range(3):
            rows = jnp.concatenate([in1[b, i, :, q * 128 : q * 128 + 128] for i in range(NX)], axis=1)
            acc[:, q * 512 : q * 512 + 512] += dot_nt(rows, scat[q, :, b * 1024 : b * 1024 + 1024])

    build(0)
    in1[:, :, COLS:80, :] = jnp.ones((4, NX, 16, 384), BF)
    ftd[0:COLS] = feat[...]
    ftd[COLS:80] = jnp.ones((16, NODES), BF)

    for half in range(2):
        took(1, half)
        pass_on(1, 2, half, up)
        took(7, half)
        pass_on(7, 6, half, down)
    arrived(idx_in.at[1], irecv.at[1])
    gather(1)
    merge_and_send(0)
    arrived(idx_in.at[7], irecv.at[7])
    gather(7)
    loads[0].wait()

    @pl.loop(0, 36)
    def _(t):
        cols = jnp.zeros((80, 128), BF)
        for q in range(NF):
            cols = jnp.where(ids[1, t] == q, ftd[:, q * 128 : q * 128 + 128], cols)
        prod[t] = dot_nt(cols, tiles[t])

    @pl.loop(0, NF)
    def _(r):
        total = jnp.zeros((80, 128), F32)
        for t in range(36):
            total = total + jnp.where(ids[0, t] == r, prod[t], 0.0)
        acc[:, pl.ds(pl.multiple_of(r * 128, 128), 128)] = total

    for half in range(2):
        took(2, half)
        pass_on(2, 3, half, up)
        took(6, half)
        pass_on(6, 5, half, down)
    arrived(idx_in.at[2], irecv.at[2])
    gather(2)
    merge_and_send(1)
    arrived(idx_in.at[6], irecv.at[6])
    gather(6)
    build(1)
    build(2)
    build(3)
    scatter(0)

    took(3, 0)
    pass_on(3, 4, 0, up)
    took(5, 0)
    took(3, 1)
    took(5, 1)
    pass_on(5, 4, 1, down)
    arrived(idx_in.at[3], irecv.at[3])
    gather(3)
    merge_and_send(2)
    arrived(idx_in.at[5], irecv.at[5])
    gather(5)

    loads[1].wait()
    for k in range(1, NF):
        arrived(frows.at[mod(f + NF - k, NF)], frecv.at[k])
    pre[...] = dot(frows[...].reshape(768, 128).T, s1[...])

    wso[CLS - 9 : CPAD] = jnp.zeros((16, HID), BF)
    wno[CLS - 9 : CPAD] = jnp.zeros((16, HID), BF)
    wso[0:CLS] = so[...]
    wno[0:CLS] = no[...]

    lane = iota((ND, 1024), 1)
    spread = (lax.div(lane, 16) == iota((ND, 1024), 0)).astype(F32).astype(BF)
    t2 = jnp.where(iota((16, ND), 0) < counts[f], targets[f], -512).astype(F32).astype(BF)
    own = iota((16, 1024), 0) == (iota((16, 1024), 1) & 15)
    t_row = jnp.sum(jnp.where(own, dot(t2, spread), 0.0), axis=0, keepdims=True).astype(I32)
    w_row = jnp.sum(jnp.where(own, dot(weights[f], spread), 0.0), axis=0, keepdims=True)
    scat2[...] = jnp.where(iota((128, 1024), 0) == t_row, w_row, 0.0).astype(BF)
    s2 = sources[f]
    high2 = (s2 >> 8).astype(F32).astype(BF)
    low2 = (s2 & 255).astype(F32).astype(BF)

    @pl.loop(0, 8)
    def _(j):
        rows = iota((128, ND), 0) + j * 128
        expand = (lax.div(rows, 16) == iota((128, ND), 1)).astype(F32).astype(BF)
        value = dot_nt(expand, high2) * 256.0 + dot_nt(expand, low2)
        mine = (iota((128, 16), 0) & 15) == iota((128, 16), 1)
        node = jnp.sum(jnp.where(mine, value, 0.0), axis=1, keepdims=True).astype(I32)
        for q in range(NF):
            oh2[pl.ds(pl.multiple_of(j * 128, 128), 128), q * 128 : q * 128 + 128] = (
                (iota((128, 128), 1) + q * 128) == node
            ).astype(F32).astype(BF)

    @pl.loop(0, NF)
    def _(q):
        block = jnp.zeros((128, 128), BF)
        for t in range(36):
            block = jnp.where((ids[0, t] == f) & (ids[1, t] == q), tiles[t], block)
        band[:, pl.ds(pl.multiple_of(q * 128, 128), 128)] = block

    z[...] = jnp.zeros((256, NODES), BF)
    scatter(1)

    took(4, 0)
    took(4, 1)
    arrived(idx_in.at[4], irecv.at[4])
    gather(4)
    merge_and_send(3)
    scatter(2)
    loads[2].wait()
    scatter(3)

    for k in range(NF):
        g = mod(f + k, NF)
        part = acc[:, pl.ds(pl.multiple_of(g * 128, 128), 128)]
        mean = (part[0:COLS] / part[COLS : COLS + 1]).astype(BF)
        if k == 0:
            nrows[f] = mean
            deg[...] = part[COLS : COLS + 8]
        else:
            nsend_buf[g] = mean
            go(remote(nsend_buf.at[g], nrows.at[f], nsend.at[k], nrecv.at[k], g, d))
    for k in range(1, NF):
        arrived(nrows.at[mod(f + NF - k, NF)], nrecv.at[k])

    hidden = jnp.maximum(pre[...] + dot(nrows[...].reshape(768, 128).T, n1[...]), 0.0).astype(BF)
    hidden_ref[...] = hidden

    def block_at(g):
        return z.at[pl.ds(0, CPAD), pl.ds(pl.multiple_of(g * 128, 128), 128)]

    z[0:CPAD, pl.ds(pl.multiple_of(f * 128, 128), 128)] = dot_nt(wno[...], hidden_ref[...]).astype(BF)

    right = mod(f + 1, NF)
    left = mod(f + NF - 1, NF)

    def ring(side, k):
        g = mod(f + NF - k, NF) if side == 0 else mod(f + k, NF)
        go(remote(
            block_at(g), block_at(g), zsend.at[side, k], zrecv.at[side, k], right if side == 0 else left, d
        ))

    ring(0, 0)
    ring(1, 0)
    own_term = dot_nt(wso[...], hidden_ref[...])
    for k in range(6):
        arrived(block_at(mod(f + NF - 1 - k, NF)), zrecv.at[0, k])
        if k < 5:
            ring(0, k + 1)
            arrived(block_at(mod(f + 1 + k, NF)), zrecv.at[1, k])
        if k < 4:
            ring(1, k + 1)

    for j in range(4):
        out2[j * 256 : j * 256 + 256] = dot_nt(oh2[j * 256 : j * 256 + 256], z[...]).astype(BF)

    @pl.loop(1, ND)
    def _(k):
        to = mod(d + k, ND)
        remote(
            out2.at[pl.ds(pl.multiple_of(to * 16, 16), 16)], in2.at[pl.ds(pl.multiple_of(d * 16, 16), 16)],
            asend, arecv, f, to,
        ).start()

    mine = pl.ds(pl.multiple_of(d * 16, 16), 16)
    in2[mine] = out2[mine]
    total = dot_nt(band[...], z[...])
    arrived(in2.at[pl.ds(0, 1008)], arecv)
    total = total + dot(scat2[...], in2[...])
    logits_ref[...] = own_term[0:CLS] + (total.T)[0:CLS] / deg[0:1]

    arrived(out2.at[pl.ds(0, 1008)], asend)
    for copy in sent:
        copy.wait_send()


def on_device(
    features, tiles, tile_ids, sources, targets, counts, edge_weight, self_one, neigh_one, self_out, neigh_out
):
    vmem = pl.BlockSpec(memory_space=pltpu.VMEM)
    anywhere = pl.BlockSpec(memory_space=pl.ANY)
    dma = pltpu.SemaphoreType.DMA
    hidden, logits = pl.pallas_call(
        kernel,
        out_shape=(jax.ShapeDtypeStruct((128, HID), BF), jax.ShapeDtypeStruct((CLS, 128), F32)),
        in_specs=[pl.BlockSpec(memory_space=pltpu.SMEM)] + [vmem] * 5 + [anywhere] * 3 + [vmem] * 2,
        out_specs=(vmem, vmem),
        scratch_shapes=[
            pltpu.VMEM((36, 128, 128), BF),
            pltpu.VMEM((768, HID), BF),
            pltpu.VMEM((768, HID), BF),
            pltpu.VMEM((NY, COLS, NODES), BF),
            pltpu.VMEM((NY, 16, 128), I32),
            pltpu.VMEM((NY, 16, 128), I32),
            pltpu.VMEM((NY, COLS, NODES), BF),
            pltpu.VMEM((4, NX, COLS, 384), BF),
            pltpu.VMEM((4, NX, 80, 384), BF),
            pltpu.VMEM((80, NODES), BF),
            pltpu.VMEM((3, 512, 4096), BF),
            pltpu.VMEM((3, 32, 128), I32),
            pltpu.VMEM((3, 32, 128), F32),
            pltpu.VMEM((80, NODES), F32),
            pltpu.VMEM((NF, COLS, 128), BF),
            pltpu.VMEM((NF, COLS, 128), BF),
            pltpu.VMEM((NF, COLS, 128), BF),
            pltpu.VMEM((128, HID), F32),
            pltpu.VMEM((CPAD, HID), BF),
            pltpu.VMEM((CPAD, HID), BF),
            pltpu.VMEM((256, NODES), BF),
            pltpu.VMEM((1024, NODES), BF),
            pltpu.VMEM((128, 1024), BF),
            pltpu.VMEM((1024, 256), BF),
            pltpu.VMEM((1024, 256), BF),
            pltpu.VMEM((8, 128), F32),
            pltpu.VMEM((36, 80, 128), F32),
            pltpu.VMEM((128, NODES), BF),
            dma((3,)),
            dma((NY, 2)), dma((NY, 2)),
            dma((NY,)), dma((NY,)),
            dma((NF,)), dma((NF,)),
            dma((4, NX)), dma((4, NX)),
            dma((NF,)), dma((NF,)),
            dma((2, 6)), dma((2, 6)),
            dma, dma,
        ],
        compiler_params=pltpu.CompilerParams(
            collective_id=0, has_side_effects=True, vmem_limit_bytes=56 * 1024 * 1024
        ),
    )(
        tile_ids[0].T,
        jnp.transpose(counts, (2, 0, 1)),
        jnp.transpose(sources[0], (1, 2, 0)),
        jnp.transpose(targets[0], (1, 2, 0)),
        jnp.transpose(edge_weight[0], (1, 2, 0)),
        features[0].T,
        tiles[0],
        self_one,
        neigh_one,
        self_out.T,
        neigh_out.T,
    )
    return hidden[None], logits[None]


def solution(mesh):
    placed = (
        P("dom", None, "feat"),
        P("dom", None, None, None),
        P("dom", None, None),
        P("dom", None, None, None),
        P("dom", None, None, None),
        P("dom", None, None),
        P("dom", None, None, None),
        P(),
        P(),
        P(),
        P(),
    )
    return jax.shard_map(
        on_device,
        mesh=mesh,
        in_specs=placed,
        out_specs=(P("dom", "feat", None), P("dom", None, "feat")),
        check_vma=False,
    )
```

```python
import jax
import jax.numpy as jnp
from jax import lax
from jax.experimental import pallas as pl
from jax.experimental.pallas import tpu as pltpu
from jax.sharding import PartitionSpec as P

MESH = pl.DeviceIdType.MESH
BF = jnp.bfloat16
F32 = jnp.float32
I32 = jnp.int32
NT = (((1,), (1,)), ((), ()))

NF = 12
ND = 64
NY = 8
NX = 8
COLS = 64
NODES = 1536
HID = 1024
CLS = 153
CPAD = 160
PAIRS = ((0, 1), (2, 7), (6, 3), (4, 5))


def iota(shape, dim):
    return lax.broadcasted_iota(I32, shape, dim)


def mod(a, n):
    return lax.rem(a, jnp.int32(n))


def dot(a, b):
    return jnp.dot(a, b, preferred_element_type=F32)


def dot_nt(a, b):
    return lax.dot_general(a, b, NT, preferred_element_type=F32)


def kernel(
    ids, counts, sources, targets, weights, feat, tiles_hbm, s1_hbm, n1_hbm, so, no,
    hidden_ref, logits_ref,
    tiles, s1, n1, tab, idx_out, idx_in, picked, out1, in1, ftd, scat, rows_t, rows_w, acc,
    frows, nsend_buf, nrows, pre, wso, wno, z, oh2, scat2, out2, in2, deg, prod, band,
    loc, tsend, trecv, isend, irecv, fsend, frecv, xsend, xrecv, nsend, nrecv, zsend, zrecv, asend, arecv,
):
    f = lax.axis_index("feat")
    d = lax.axis_index("dom")
    y = lax.div(d, jnp.int32(NX))
    xc = mod(d, NX)
    core = mod(d, 2)

    loads = [
        pltpu.make_async_copy(tiles_hbm, tiles, loc.at[0]),
        pltpu.make_async_copy(s1_hbm, s1, loc.at[1]),
        pltpu.make_async_copy(n1_hbm, n1, loc.at[2]),
    ]
    for load in loads:
        load.start()

    def remote(src, dst, ss, rs, fi, di):
        return pltpu.make_async_remote_copy(
            src_ref=src, dst_ref=dst, send_sem=ss, recv_sem=rs, device_id=(fi, di), device_id_type=MESH
        )

    def arrived(dst, rs):
        pltpu.make_async_copy(dst, dst, rs).wait()

    def row_peer(k):
        return mod(y + k, NY) * NX + xc

    def col_peer(k):
        return y * NX + mod(xc + k, NX)

    barrier = pltpu.get_barrier_semaphore()
    for k in range(1, NY):
        pl.semaphore_signal(barrier, inc=1, device_id=(f, row_peer(k)), device_id_type=MESH)
    for k in range(1, NX):
        pl.semaphore_signal(barrier, inc=1, device_id=(f, col_peer(k)), device_id_type=MESH)
    for k in range(1, NF):
        pl.semaphore_signal(barrier, inc=1, device_id=(mod(f + k, NF), d), device_id_type=MESH)

    src = sources[...].reshape(192, ND)
    both = jnp.concatenate([src >> 8, src & 255], axis=0).astype(F32).astype(BF)
    r32 = iota((32, ND), 0)
    e32 = iota((32, ND), 1)
    flip = (lax.div(r32, 4) + y) & 1
    halves = []
    for h in range(2):
        pick = (e32 == r32 * 2 + (flip ^ h)).astype(F32).astype(BF)
        got = dot_nt(pick, both)
        halves.append((got[:, :192] * 256.0 + got[:, 192:]).astype(I32))
    for q in range(3):
        tile = jnp.concatenate([halves[0][:, q * 64 : q * 64 + 64], halves[1][:, q * 64 : q * 64 + 64]], axis=1)
        for row in range(NY):
            idx_out[row, q * 4 : q * 4 + 4, :] = tile[row * 4 : row * 4 + 4]
    idx_in[0] = idx_out[y]

    pl.semaphore_wait(barrier, NY - 1 + NX - 1 + NF - 1)

    sent = []

    def go(copy):
        copy.start()
        sent.append(copy)

    def table(slot):
        return feat if slot == 0 else tab.at[slot]

    def pass_on(from_slot, to_slot, half, di):
        part = pl.ds(half * 768, 768)
        go(remote(
            table(from_slot).at[:, part], tab.at[to_slot, :, part],
            tsend.at[to_slot, half], trecv.at[to_slot, half], f, di,
        ))

    def took(slot, half):
        arrived(tab.at[slot, :, pl.ds(half * 768, 768)], trecv.at[slot, half])

    up = row_peer(1)
    down = row_peer(NY - 1)
    for half in range(2):
        pass_on(0, 1, half, up)
        pass_on(0, 7, half, down)
    for k in range(1, NY):
        to = mod(y + k, NY)
        go(remote(idx_out.at[to], idx_in.at[k], isend.at[k], irecv.at[k], f, to * NX + xc))
    for k in range(1, NF):
        g = mod(f + k, NF)
        go(remote(
            feat.at[:, pl.ds(pl.multiple_of(g * 128, 128), 128)], frows.at[f], fsend.at[k], frecv.at[k], g, d
        ))
    frows[f] = feat[:, pl.ds(pl.multiple_of(f * 128, 128), 128)]

    def gather(slot):
        here = table(slot)
        for r in range(6):
            wide = jnp.concatenate([here[:, k * 256 : k * 256 + 256] for k in range(6)], axis=0)
            pick = jnp.concatenate(
                [idx_in[slot, 2 * r : 2 * r + 1, :], idx_in[slot, 2 * r + 1 : 2 * r + 2, :]], axis=1
            )
            low = pick & 255
            high = pick >> 8
            one_hot = (iota((256, 256), 0) == low).astype(F32).astype(BF)
            got = dot(wide, one_hot)
            kept = jnp.zeros((COLS, 256), F32)
            for k in range(6):
                kept = jnp.where(high == k, got[k * COLS : k * COLS + COLS], kept)
            picked[slot, :, r * 256 : r * 256 + 256] = kept.astype(BF)

    first_half = iota((COLS, 128), 1) < 64

    def merge(b, q):
        even, odd = PAIRS[b]
        for col in range(4):
            at = (q * 4 + col) * 128
            one = picked[even, :, at : at + 128]
            two = picked[odd, :, at : at + 128]
            out1[b, 2 * col, :, q * 128 : q * 128 + 128] = jnp.where(first_half, one, two)
            out1[b, 2 * col + 1, :, q * 128 : q * 128 + 128] = jnp.where(first_half, two, one)

    def merge_and_send(b):
        for q in range(3):
            merge(b, q)
        for k in (4, 3, 5, 2, 6, 1, 7):
            to = mod(xc + k, NX)
            go(remote(
                out1.at[b, to], in1.at[b, xc, pl.ds(0, COLS)], xsend.at[b, k], xrecv.at[b, k], f, y * NX + to
            ))
        in1[b, xc, 0:COLS] = out1[b, xc]

    def last_batch(q):
        merge(3, q)
        part = pl.ds(q * 128, 128)
        for k in (4, 3, 5, 2, 6, 1, 7):
            to = mod(xc + k, NX)
            go(remote(
                out1.at[3, to, :, part], in1.at[3, xc, pl.ds(0, COLS), part],
                xsend.at[3 + q, k], xrecv.at[3 + q, k], f, y * NX + to,
            ))
        in1[3, xc, 0:COLS, part] = out1[3, xc, :, part]

    gather(0)

    live = iota((NF, 16, ND), 1) < counts[...]
    t_all = jnp.where(live, targets[...], -512).reshape(192, ND)
    w_all = weights[...].reshape(192, ND)
    both = jnp.concatenate([t_all.astype(F32).astype(BF), w_all], axis=0)
    batch = lax.div(r32, 8)
    halves = []
    for h in range(2):
        par = core ^ h
        far = jnp.zeros((32, ND), I32)
        for b in range(4):
            dist = jnp.where(par == 0, PAIRS[b][0], PAIRS[b][1])
            far = jnp.where(batch == b, dist, far)
        origin = ((y + 8 - far) & 7) * 8 + (r32 & 7)
        halves.append(dot_nt((e32 == origin).astype(F32).astype(BF), both))
    for q in range(3):
        lanes = iota((32, 128), 1)
        base = (lax.div(lanes, 16) & 3) * 128
        t_tile = jnp.concatenate([halves[0][:, q * 64 : q * 64 + 64], halves[1][:, q * 64 : q * 64 + 64]], axis=1)
        w_tile = jnp.concatenate(
            [halves[0][:, 192 + q * 64 : 256 + q * 64], halves[1][:, 192 + q * 64 : 256 + q * 64]], axis=1
        )
        rows_t[q] = t_tile.astype(I32) + base
        rows_w[q] = w_tile

    def build(b):
        @pl.loop(0, 8)
        def _(i):
            r = b * 8 + i
            for q in range(3):
                t = rows_t[q, pl.ds(r, 1), :]
                w = rows_w[q, pl.ds(r, 1), :]
                scat[q, :, pl.ds(pl.multiple_of(r * 128, 128), 128)] = jnp.where(
                    iota((512, 128), 0) == t, w, 0.0
                ).astype(BF)

    def scatter_part(b, q):
        rows = jnp.concatenate([in1[b, i, :, q * 128 : q * 128 + 128] for i in range(NX)], axis=1)
        acc[:, q * 512 : q * 512 + 512] += dot_nt(rows, scat[q, :, b * 1024 : b * 1024 + 1024])

    def arrive_batch(b):
        for k in range(1, NX):
            arrived(in1.at[b, mod(xc + NX - k, NX), pl.ds(0, COLS)], xrecv.at[b, k])

    def scatter(b):
        arrive_batch(b)
        for q in range(3):
            scatter_part(b, q)

    build(0)
    build(1)
    in1[:, :, COLS:80, :] = jnp.ones((4, NX, 16, 384), BF)
    z[CPAD:256] = jnp.zeros((256 - CPAD, NODES), BF)
    ftd[0:COLS] = feat[...]
    ftd[COLS:80] = jnp.ones((16, NODES), BF)

    took(1, 0)
    pass_on(1, 2, 0, up)
    took(7, 0)
    pass_on(7, 6, 0, down)
    build(2)
    took(1, 1)
    pass_on(1, 2, 1, up)
    took(7, 1)
    pass_on(7, 6, 1, down)
    arrived(idx_in.at[1], irecv.at[1])
    gather(1)
    merge_and_send(0)
    loads[0].wait()

    @pl.loop(0, 6)
    def _(r):
        for i in range(6):
            t = r * 6 + i
            cols = jnp.zeros((80, 128), BF)
            for q in range(NF):
                cols = jnp.where(ids[1, t] == q, ftd[:, q * 128 : q * 128 + 128], cols)
            prod[t] = dot_nt(cols, tiles[t])

    took(2, 0)
    pass_on(2, 3, 0, up)
    took(6, 0)
    pass_on(6, 5, 0, down)
    arrived(idx_in.at[7], irecv.at[7])
    gather(7)
    build(3)
    took(2, 1)
    pass_on(2, 3, 1, up)
    took(6, 1)
    pass_on(6, 5, 1, down)
    arrived(idx_in.at[2], irecv.at[2])
    gather(2)
    merge_and_send(1)

    @pl.loop(0, NF)
    def _(r):
        total = jnp.zeros((80, 128), F32)
        for t in range(36):
            total = total + jnp.where(ids[0, t] == r, prod[t], 0.0)
        acc[:, pl.ds(pl.multiple_of(r * 128, 128), 128)] = total

    took(3, 0)
    pass_on(3, 4, 0, up)
    took(5, 0)
    arrived(idx_in.at[6], irecv.at[6])
    gather(6)
    took(3, 1)
    took(5, 1)
    pass_on(5, 4, 1, down)
    arrived(idx_in.at[3], irecv.at[3])
    gather(3)
    merge_and_send(2)
    arrived(idx_in.at[5], irecv.at[5])
    gather(5)
    scatter(0)
    took(4, 0)
    took(4, 1)
    arrived(idx_in.at[4], irecv.at[4])
    gather(4)
    for q in range(3):
        last_batch(q)

    scatter(1)
    scatter(2)
    loads[1].wait()
    for k in range(1, NF):
        arrived(frows.at[mod(f + NF - k, NF)], frecv.at[k])
    pre[...] = dot(frows[...].reshape(768, 128).T, s1[...])
    for q in range(3):
        for k in range(1, NX):
            arrived(in1.at[3, mod(xc + NX - k, NX), pl.ds(0, COLS), pl.ds(q * 128, 128)], xrecv.at[3 + q, k])
        scatter_part(3, q)
        for g in range(q * 4, q * 4 + 4):
            part = acc[:, g * 128 : g * 128 + 128]
            nsend_buf[g] = (part[0:COLS] / part[COLS : COLS + 1]).astype(BF)

            @pl.when(f != g)
            def _():
                remote(nsend_buf.at[g], nrows.at[f], nsend.at[g], nrecv.at[f], g, d).start()

    nrows[f] = nsend_buf[f]
    deg[...] = acc[COLS : COLS + 8, pl.ds(pl.multiple_of(f * 128, 128), 128)]
    loads[2].wait()
    wno[CLS - 9 : CPAD] = jnp.zeros((16, HID), BF)
    wno[0:CLS] = no[...]
    s2 = sources[f]
    high2 = (s2 >> 8).astype(F32).astype(BF)
    low2 = (s2 & 255).astype(F32).astype(BF)

    @pl.loop(0, 8)
    def _(j):
        rows = iota((128, ND), 0) + j * 128
        expand = (lax.div(rows, 16) == iota((128, ND), 1)).astype(F32).astype(BF)
        value = dot_nt(expand, high2) * 256.0 + dot_nt(expand, low2)
        mine = (iota((128, 16), 0) & 15) == iota((128, 16), 1)
        node = jnp.sum(jnp.where(mine, value, 0.0), axis=1, keepdims=True).astype(I32)
        for q in range(NF):
            oh2[pl.ds(pl.multiple_of(j * 128, 128), 128), q * 128 : q * 128 + 128] = (
                (iota((128, 128), 1) + q * 128) == node
            ).astype(F32).astype(BF)

    for k in range(1, NF):
        g = mod(f + NF - k, NF)
        arrived(nrows.at[g], nrecv.at[g])

    hidden = jnp.maximum(pre[...] + dot(nrows[...].reshape(768, 128).T, n1[...]), 0.0).astype(BF)
    hidden_ref[...] = hidden

    def block_at(g):
        return z.at[pl.ds(0, CPAD), pl.ds(pl.multiple_of(g * 128, 128), 128)]

    z[0:CPAD, pl.ds(pl.multiple_of(f * 128, 128), 128)] = dot_nt(wno[...], hidden_ref[...]).astype(BF)

    way = 1 - 2 * core
    ways = (way, -way)

    def from_far(side, k):
        return block_at(mod(f + NF - ways[side] * k, NF))

    def throw(side, held, hops):
        block = from_far(side, held)
        k = held + hops
        go(remote(block, block, zsend.at[side, k], zrecv.at[side, k], mod(f + NF + ways[side] * hops, NF), d))

    def caught(side, k):
        arrived(from_far(side, k), zrecv.at[side, k])

    for hops in (4, 2, 1):
        for side in range(2):
            throw(side, 0, hops)
    caught(0, 4)
    throw(0, 4, 2)
    throw(0, 4, 1)
    caught(1, 4)
    throw(1, 4, 1)
    for side in range(2):
        caught(side, 2)
        throw(side, 2, 1)

    wso[CLS - 9 : CPAD] = jnp.zeros((16, HID), BF)
    wso[0:CLS] = so[...]
    own_term = dot_nt(wso[...], hidden_ref[...])
    lane = iota((ND, 1024), 1)
    spread = (lax.div(lane, 16) == iota((ND, 1024), 0)).astype(F32).astype(BF)
    t2 = jnp.where(iota((16, ND), 0) < counts[f], targets[f], -512).astype(F32).astype(BF)
    own = iota((16, 1024), 0) == (iota((16, 1024), 1) & 15)
    t_row = jnp.sum(jnp.where(own, dot(t2, spread), 0.0), axis=0, keepdims=True).astype(I32)
    w_row = jnp.sum(jnp.where(own, dot(weights[f], spread), 0.0), axis=0, keepdims=True)
    scat2[...] = jnp.where(iota((128, 1024), 0) == t_row, w_row, 0.0).astype(BF)

    @pl.loop(0, NF)
    def _(q):
        block = jnp.zeros((128, 128), BF)
        for t in range(36):
            block = jnp.where((ids[0, t] == f) & (ids[1, t] == q), tiles[t], block)
        band[:, pl.ds(pl.multiple_of(q * 128, 128), 128)] = block

    for k in (1, 3, 5):
        caught(0, k)
        caught(1, k)
    caught(0, 6)

    for j in range(4):
        base = mod(lax.div(d, 16) + j, 4) * 16
        rows = pl.ds(pl.multiple_of(base * 16, 256), 256)
        out2[rows] = dot_nt(oh2[rows], z[...]).astype(BF)

        @pl.loop(0, 16)
        def _(k):
            to = base + mod(d + k, 16)

            @pl.when(to != d)
            def _():
                remote(
                    out2.at[pl.ds(pl.multiple_of(to * 16, 16), 16)], in2.at[pl.ds(pl.multiple_of(d * 16, 16), 16)],
                    asend, arecv, f, to,
                ).start()

    mine = pl.ds(pl.multiple_of(d * 16, 16), 16)
    in2[mine] = out2[mine]
    total = dot_nt(band[...], z[...])
    arrived(in2.at[pl.ds(0, 1008)], arecv)
    total = total + dot(scat2[...], in2[...])
    logits_ref[:, 0, :] = own_term[0:CLS] + (total.T)[0:CLS] / deg[0:1]

    arrived(out2.at[pl.ds(0, 1008)], asend)
    for k in range(1, NF):
        g = mod(f + k, NF)
        arrived(nsend_buf.at[g], nsend.at[g])
    for copy in sent:
        copy.wait_send()


def hand_over(hidden_ref, logits_ref, hidden_out, logits_out):
    hidden_out[...] = hidden_ref[...]
    logits_out[...] = logits_ref[...]


def on_device(
    features, tiles, tile_ids, sources, targets, counts, edge_weight, self_one, neigh_one, self_out, neigh_out
):
    vmem = pl.BlockSpec(memory_space=pltpu.VMEM)
    anywhere = pl.BlockSpec(memory_space=pl.ANY)
    dma = pltpu.SemaphoreType.DMA
    hidden, logits = pl.pallas_call(
        kernel,
        out_shape=(jax.ShapeDtypeStruct((128, HID), BF), jax.ShapeDtypeStruct((CLS, 1, 128), F32)),
        in_specs=[pl.BlockSpec(memory_space=pltpu.SMEM)] + [vmem] * 5 + [anywhere] * 3 + [vmem] * 2,
        out_specs=(vmem, vmem),
        scratch_shapes=[
            pltpu.VMEM((36, 128, 128), BF),
            pltpu.VMEM((768, HID), BF),
            pltpu.VMEM((768, HID), BF),
            pltpu.VMEM((NY, COLS, NODES), BF),
            pltpu.VMEM((NY, 16, 128), I32),
            pltpu.VMEM((NY, 16, 128), I32),
            pltpu.VMEM((NY, COLS, NODES), BF),
            pltpu.VMEM((4, NX, COLS, 384), BF),
            pltpu.VMEM((4, NX, 80, 384), BF),
            pltpu.VMEM((80, NODES), BF),
            pltpu.VMEM((3, 512, 4096), BF),
            pltpu.VMEM((3, 32, 128), I32),
            pltpu.VMEM((3, 32, 128), F32),
            pltpu.VMEM((80, NODES), F32),
            pltpu.VMEM((NF, COLS, 128), BF),
            pltpu.VMEM((NF, COLS, 128), BF),
            pltpu.VMEM((NF, COLS, 128), BF),
            pltpu.VMEM((128, HID), F32),
            pltpu.VMEM((CPAD, HID), BF),
            pltpu.VMEM((CPAD, HID), BF),
            pltpu.VMEM((256, NODES), BF),
            pltpu.VMEM((1024, NODES), BF),
            pltpu.VMEM((128, 1024), BF),
            pltpu.VMEM((1024, 256), BF),
            pltpu.VMEM((1024, 256), BF),
            pltpu.VMEM((8, 128), F32),
            pltpu.VMEM((36, 80, 128), F32),
            pltpu.VMEM((128, NODES), BF),
            dma((3,)),
            dma((NY, 2)), dma((NY, 2)),
            dma((NY,)), dma((NY,)),
            dma((NF,)), dma((NF,)),
            dma((6, NX)), dma((6, NX)),
            dma((NF,)), dma((NF,)),
            dma((2, 7)), dma((2, 7)),
            dma, dma,
        ],
        compiler_params=pltpu.CompilerParams(
            collective_id=0, has_side_effects=True, vmem_limit_bytes=56 * 1024 * 1024
        ),
    )(
        tile_ids[0].T,
        jnp.transpose(counts, (2, 0, 1)),
        jnp.transpose(sources[0], (1, 2, 0)),
        jnp.transpose(targets[0], (1, 2, 0)),
        jnp.transpose(edge_weight[0], (1, 2, 0)),
        features[0].T,
        tiles[0],
        self_one,
        neigh_one,
        self_out.T,
        neigh_out.T,
    )
    hidden, logits = pl.pallas_call(
        hand_over,
        out_shape=(jax.ShapeDtypeStruct((128, HID), BF), jax.ShapeDtypeStruct((CLS, 1, 128), F32)),
        in_specs=[vmem] * 2,
        out_specs=(vmem, vmem),
    )(hidden, logits)
    return hidden[None], jnp.transpose(logits, (1, 0, 2))


def solution(mesh):
    placed = (
        P("dom", None, "feat"),
        P("dom", None, None, None),
        P("dom", None, None),
        P("dom", None, None, None),
        P("dom", None, None, None),
        P("dom", None, None),
        P("dom", None, None, None),
        P(),
        P(),
        P(),
        P(),
    )
    return jax.shard_map(
        on_device,
        mesh=mesh,
        in_specs=placed,
        out_specs=(P("dom", "feat", None), P("dom", None, "feat")),
        check_vma=False,
    )
```

```python
import jax
import jax.numpy as jnp
from jax import lax
from jax.experimental import pallas as pl
from jax.experimental.pallas import tpu as pltpu
from jax.sharding import PartitionSpec as P

MESH = pl.DeviceIdType.MESH
BF = jnp.bfloat16
F32 = jnp.float32
I32 = jnp.int32
NT = (((1,), (1,)), ((), ()))

NF = 12
ND = 64
NY = 8
NX = 8
COLS = 64
NODES = 1536
HID = 1024
CLS = 153
CPAD = 160
PAIRS = ((0, 1), (2, 7), (6, 3), (4, 5))


def iota(shape, dim):
    return lax.broadcasted_iota(I32, shape, dim)


def mod(a, n):
    return lax.rem(a, jnp.int32(n))


def dot(a, b):
    return jnp.dot(a, b, preferred_element_type=F32)


def dot_nt(a, b):
    return lax.dot_general(a, b, NT, preferred_element_type=F32)


def kernel(
    ids, counts_hbm, sources_hbm, targets_hbm, weights_hbm, feat_hbm, tiles_hbm, s1_hbm, n1_hbm, so_hbm, no_hbm,
    hidden_ref, logits_ref,
    counts, sources, targets, weights, feat, so, no, tiles, s1, n1, tab, idx_out, idx_in, picked, out1, in1, ftd, scat, rows_t, rows_w, acc,
    frows, nsend_buf, nrows, pre, wso, wno, z, oh2, scat2, out2, in2, deg, prod, band, outb, inb, outb2, inb2,
    loc, tsend, trecv, isend, irecv, fsend, frecv, xsend, xrecv, nsend, nrecv, zsend, zrecv, asend, arecv, bsend, brecv,
):
    f = lax.axis_index("feat")
    d = lax.axis_index("dom")
    y = lax.div(d, jnp.int32(NX))
    xc = mod(d, NX)
    core = mod(d, 2)

    def remote(src, dst, ss, rs, fi, di):
        return pltpu.make_async_remote_copy(
            src_ref=src, dst_ref=dst, send_sem=ss, recv_sem=rs, device_id=(fi, di), device_id_type=MESH
        )

    def arrived(dst, rs):
        pltpu.make_async_copy(dst, dst, rs).wait()

    def row_peer(k):
        return mod(y + k, NY) * NX + xc

    def col_peer(k):
        return y * NX + mod(xc + k, NX)

    barrier = pltpu.get_barrier_semaphore()
    for k in range(1, NY):
        pl.semaphore_signal(barrier, inc=1, device_id=(f, row_peer(k)), device_id_type=MESH)
    for k in range(1, NX):
        pl.semaphore_signal(barrier, inc=1, device_id=(f, col_peer(k)), device_id_type=MESH)
    for k in range(1, NF):
        pl.semaphore_signal(barrier, inc=1, device_id=(mod(f + k, NF), d), device_id_type=MESH)

    loads = [
        pltpu.make_async_copy(far, near, loc.at[i])
        for i, (far, near) in enumerate((
            (sources_hbm, sources), (feat_hbm, feat), (targets_hbm, targets), (counts_hbm, counts),
            (weights_hbm, weights), (tiles_hbm, tiles), (s1_hbm, s1), (n1_hbm, n1), (no_hbm, no), (so_hbm, so),
        ))
    ]
    for load in loads:
        load.start()

    spread_out = [place * 3 + third for third in range(3) for place in range(4)]

    loads[0].wait()
    src = jnp.concatenate([sources[g] for g in spread_out], axis=0)
    both = jnp.concatenate([src >> 8, src & 255], axis=0).astype(F32).astype(BF)
    r32 = iota((32, ND), 0)
    e32 = iota((32, ND), 1)
    flip = (lax.div(r32, 4) + y) & 1
    halves = []
    for h in range(2):
        pick = (e32 == r32 * 2 + (flip ^ h)).astype(F32).astype(BF)
        got = dot_nt(pick, both)
        halves.append((got[:, :192] * 256.0 + got[:, 192:]).astype(I32))
    for q in range(3):
        tile = jnp.concatenate([halves[0][:, q * 64 : q * 64 + 64], halves[1][:, q * 64 : q * 64 + 64]], axis=1)
        for row in range(NY):
            idx_out[row, q * 4 : q * 4 + 4, :] = tile[row * 4 : row * 4 + 4]
    idx_in[0] = idx_out[y]

    loads[1].wait()
    pl.semaphore_wait(barrier, NY - 1 + NX - 1 + NF - 1)

    sent = []

    def go(copy):
        copy.start()
        sent.append(copy)

    def table(slot):
        return feat if slot == 0 else tab.at[slot]

    def pass_on(from_slot, to_slot, half, di):
        part = pl.ds(half * 768, 768)
        go(remote(
            table(from_slot).at[:, part], tab.at[to_slot, :, part],
            tsend.at[to_slot, half], trecv.at[to_slot, half], f, di,
        ))

    def took(slot, half):
        arrived(tab.at[slot, :, pl.ds(half * 768, 768)], trecv.at[slot, half])

    up = row_peer(1)
    down = row_peer(NY - 1)
    for half in range(2):
        pass_on(0, 1, half, up)
        pass_on(0, 7, half, down)
    for k in range(1, NY):
        to = mod(y + k, NY)
        go(remote(idx_out.at[to], idx_in.at[k], isend.at[k], irecv.at[k], f, to * NX + xc))
    for k in range(1, NF):
        g = mod(f + k, NF)
        go(remote(
            feat.at[:, pl.ds(pl.multiple_of(g * 128, 128), 128)], frows.at[f], fsend.at[k], frecv.at[k], g, d
        ))
    frows[f] = feat[:, pl.ds(pl.multiple_of(f * 128, 128), 128)]

    def gather(slot):
        here = table(slot)
        for r in range(6):
            wide = jnp.concatenate([here[:, k * 256 : k * 256 + 256] for k in range(6)], axis=0)
            pick = jnp.concatenate(
                [idx_in[slot, 2 * r : 2 * r + 1, :], idx_in[slot, 2 * r + 1 : 2 * r + 2, :]], axis=1
            )
            low = pick & 255
            high = pick >> 8
            one_hot = (iota((256, 256), 0) == low).astype(F32).astype(BF)
            got = dot(wide, one_hot)
            kept = jnp.zeros((COLS, 256), F32)
            for k in range(6):
                kept = jnp.where(high == k, got[k * COLS : k * COLS + COLS], kept)
            picked[slot, :, r * 256 : r * 256 + 256] = kept.astype(BF)

    first_half = iota((COLS, 128), 1) < 64

    def merge(b, q):
        even, odd = PAIRS[b]
        for col in range(4):
            at = (q * 4 + col) * 128
            one = picked[even, :, at : at + 128]
            two = picked[odd, :, at : at + 128]
            out1[b, 2 * col, :, q * 128 : q * 128 + 128] = jnp.where(first_half, one, two)
            out1[b, 2 * col + 1, :, q * 128 : q * 128 + 128] = jnp.where(first_half, two, one)

    def merge_and_send(b):
        for q in range(3):
            merge(b, q)
        for k in (4, 3, 5, 2, 6, 1, 7):
            to = mod(xc + k, NX)
            go(remote(
                out1.at[b, to], in1.at[b, xc, pl.ds(0, COLS)], xsend.at[b, k], xrecv.at[b, k], f, y * NX + to
            ))
        in1[b, xc, 0:COLS] = out1[b, xc]

    def last_batch(q):
        merge(3, q)
        part = pl.ds(q * 128, 128)
        for k in (4, 3, 5, 2, 6, 1, 7):
            to = mod(xc + k, NX)
            go(remote(
                out1.at[3, to, :, part], in1.at[3, xc, pl.ds(0, COLS), part],
                xsend.at[3 + q, k], xrecv.at[3 + q, k], f, y * NX + to,
            ))
        in1[3, xc, 0:COLS, part] = out1[3, xc, :, part]

    gather(0)

    for i in (2, 3, 4):
        loads[i].wait()
    t_all = jnp.concatenate(
        [jnp.where(iota((16, ND), 0) < counts[g], targets[g], -512) for g in spread_out], axis=0
    )
    w_all = jnp.concatenate([weights[g] for g in spread_out], axis=0)
    both = jnp.concatenate([t_all.astype(F32).astype(BF), w_all], axis=0)
    batch = lax.div(r32, 8)
    halves = []
    for h in range(2):
        par = core ^ h
        far = jnp.zeros((32, ND), I32)
        for b in range(4):
            dist = jnp.where(par == 0, PAIRS[b][0], PAIRS[b][1])
            far = jnp.where(batch == b, dist, far)
        origin = ((y + 8 - far) & 7) * 8 + (r32 & 7)
        halves.append(dot_nt((e32 == origin).astype(F32).astype(BF), both))
    for q in range(3):
        lanes = iota((32, 128), 1)
        base = (lax.div(lanes, 16) & 3) * 128
        t_tile = jnp.concatenate([halves[0][:, q * 64 : q * 64 + 64], halves[1][:, q * 64 : q * 64 + 64]], axis=1)
        w_tile = jnp.concatenate(
            [halves[0][:, 192 + q * 64 : 256 + q * 64], halves[1][:, 192 + q * 64 : 256 + q * 64]], axis=1
        )
        rows_t[q] = t_tile.astype(I32) + base
        rows_w[q] = w_tile

    def build(b):
        @pl.loop(0, 8)
        def _(i):
            r = b * 8 + i
            for q in range(3):
                t = rows_t[q, pl.ds(r, 1), :]
                w = rows_w[q, pl.ds(r, 1), :]
                scat[q, :, pl.ds(pl.multiple_of(r * 128, 128), 128)] = jnp.where(
                    iota((512, 128), 0) == t, w, 0.0
                ).astype(BF)

    def scatter_part(b, q):
        rows = jnp.concatenate([in1[b, i, :, q * 128 : q * 128 + 128] for i in range(NX)], axis=1)
        acc[:, q * 512 : q * 512 + 512] += dot_nt(rows, scat[q, :, b * 1024 : b * 1024 + 1024])

    def arrive_batch(b):
        for k in range(1, NX):
            arrived(in1.at[b, mod(xc + NX - k, NX), pl.ds(0, COLS)], xrecv.at[b, k])

    def scatter(b):
        arrive_batch(b)
        for q in range(3):
            scatter_part(b, q)

    build(0)
    build(1)
    in1[:, :, COLS:80, :] = jnp.ones((4, NX, 16, 384), BF)
    z[CPAD:256] = jnp.zeros((256 - CPAD, NODES), BF)
    ftd[0:COLS] = feat[...]
    ftd[COLS:80] = jnp.ones((16, NODES), BF)

    took(1, 0)
    pass_on(1, 2, 0, up)
    took(7, 0)
    pass_on(7, 6, 0, down)
    build(2)
    took(1, 1)
    pass_on(1, 2, 1, up)
    took(7, 1)
    pass_on(7, 6, 1, down)
    arrived(idx_in.at[1], irecv.at[1])
    gather(1)
    merge_and_send(0)
    loads[5].wait()

    @pl.loop(0, 6)
    def _(r):
        for i in range(6):
            t = r * 6 + i
            cols = jnp.zeros((80, 128), BF)
            for q in range(NF):
                cols = jnp.where(ids[1, t] == q, ftd[:, q * 128 : q * 128 + 128], cols)
            prod[t] = dot_nt(cols, tiles[t])

    took(2, 0)
    pass_on(2, 3, 0, up)
    took(6, 0)
    pass_on(6, 5, 0, down)
    arrived(idx_in.at[7], irecv.at[7])
    gather(7)
    build(3)
    took(2, 1)
    pass_on(2, 3, 1, up)
    took(6, 1)
    pass_on(6, 5, 1, down)
    arrived(idx_in.at[2], irecv.at[2])
    gather(2)
    merge_and_send(1)

    @pl.loop(0, NF)
    def _(p):
        r = mod(p, 4) * 3 + lax.div(p, 4)
        total = jnp.zeros((80, 128), F32)
        for t in range(36):
            total = total + jnp.where(ids[0, t] == r, prod[t], 0.0)
        acc[:, pl.ds(pl.multiple_of(p * 128, 128), 128)] = total

    took(3, 0)
    pass_on(3, 4, 0, up)
    took(5, 0)
    arrived(idx_in.at[6], irecv.at[6])
    gather(6)
    took(3, 1)
    took(5, 1)
    pass_on(5, 4, 1, down)
    arrived(idx_in.at[3], irecv.at[3])
    gather(3)
    merge_and_send(2)
    arrived(idx_in.at[5], irecv.at[5])
    gather(5)
    scatter(0)
    took(4, 0)
    took(4, 1)
    arrived(idx_in.at[4], irecv.at[4])
    gather(4)
    for q in range(3):
        last_batch(q)

    scatter(1)
    scatter(2)
    loads[6].wait()
    for k in range(1, NF):
        arrived(frows.at[mod(f + NF - k, NF)], frecv.at[k])
    pre[...] = dot(frows[...].reshape(768, 128).T, s1[...])
    for q in range(3):
        for k in range(1, NX):
            arrived(in1.at[3, mod(xc + NX - k, NX), pl.ds(0, COLS), pl.ds(q * 128, 128)], xrecv.at[3 + q, k])
        scatter_part(3, q)
        for i in range(4):
            place = mod(lax.div(f, 3) + i, 4)
            g = place * 3 + q
            part = acc[:, pl.ds(pl.multiple_of(q * 512 + place * 128, 128), 128)]
            nsend_buf[g] = (part[0:COLS] / part[COLS : COLS + 1]).astype(BF)

            @pl.when(f != g)
            def _():
                remote(nsend_buf.at[g], nrows.at[f], nsend.at[g], nrecv.at[f], g, d).start()

    nrows[f] = nsend_buf[f]
    deg[...] = acc[COLS : COLS + 8, pl.ds(pl.multiple_of(mod(f, 3) * 512 + lax.div(f, 3) * 128, 128), 128)]
    loads[7].wait()
    loads[8].wait()
    wno[CLS - 9 : CPAD] = jnp.zeros((16, HID), BF)
    wno[0:CLS] = no[...]
    s2 = sources[f]
    high2 = (s2 >> 8).astype(F32).astype(BF)
    low2 = (s2 & 255).astype(F32).astype(BF)

    @pl.loop(0, 8)
    def _(j):
        rows = iota((128, ND), 0) + j * 128
        expand = (lax.div(rows, 16) == iota((128, ND), 1)).astype(F32).astype(BF)
        value = dot_nt(expand, high2) * 256.0 + dot_nt(expand, low2)
        mine = (iota((128, 16), 0) & 15) == iota((128, 16), 1)
        node = jnp.sum(jnp.where(mine, value, 0.0), axis=1, keepdims=True).astype(I32)
        for q in range(NF):
            oh2[pl.ds(pl.multiple_of(j * 128, 128), 128), q * 128 : q * 128 + 128] = (
                (iota((128, 128), 1) + q * 128) == node
            ).astype(F32).astype(BF)

    for k in range(1, NF):
        g = mod(f + NF - k, NF)
        arrived(nrows.at[g], nrecv.at[g])

    hidden = jnp.maximum(pre[...] + dot(nrows[...].reshape(768, 128).T, n1[...]), 0.0).astype(BF)
    hidden_ref[...] = hidden

    def block_at(g):
        return z.at[pl.ds(0, CPAD), pl.ds(pl.multiple_of(g * 128, 128), 128)]

    z[0:CPAD, pl.ds(pl.multiple_of(f * 128, 128), 128)] = dot_nt(wno[...], hidden_ref[...]).astype(BF)

    way = 1 - 2 * core
    ways = (way, -way)

    def from_far(side, k):
        return block_at(mod(f + NF - ways[side] * k, NF))

    def throw(side, held, hops):
        block = from_far(side, held)
        k = held + hops
        go(remote(block, block, zsend.at[side, k], zrecv.at[side, k], mod(f + NF + ways[side] * hops, NF), d))

    def caught(side, k):
        arrived(from_far(side, k), zrecv.at[side, k])

    for hops in (4, 2, 1):
        for side in range(2):
            throw(side, 0, hops)
    caught(0, 4)
    throw(0, 4, 2)
    throw(0, 4, 1)
    caught(1, 4)
    throw(1, 4, 1)
    for side in range(2):
        caught(side, 2)
        throw(side, 2, 1)

    loads[9].wait()
    wso[CLS - 9 : CPAD] = jnp.zeros((16, HID), BF)
    wso[0:CLS] = so[...]
    own_term = dot_nt(wso[...], hidden_ref[...])
    lane = iota((ND, 1024), 1)
    spread = (lax.div(lane, 16) == iota((ND, 1024), 0)).astype(F32).astype(BF)
    t2 = jnp.where(iota((16, ND), 0) < counts[f], targets[f], -512).astype(F32).astype(BF)
    own = iota((16, 1024), 0) == (iota((16, 1024), 1) & 15)
    t_row = jnp.sum(jnp.where(own, dot(t2, spread), 0.0), axis=0, keepdims=True).astype(I32)
    w_row = jnp.sum(jnp.where(own, dot(weights[f], spread), 0.0), axis=0, keepdims=True)
    scat2[...] = jnp.where(iota((128, 1024), 0) == t_row, w_row, 0.0).astype(BF)

    @pl.loop(0, NF)
    def _(q):
        block = jnp.zeros((128, 128), BF)
        for t in range(36):
            block = jnp.where((ids[0, t] == f) & (ids[1, t] == q), tiles[t], block)
        band[:, pl.ds(pl.multiple_of(q * 128, 128), 128)] = block

    for k in (1, 3, 5):
        caught(0, k)
        caught(1, k)
    caught(0, 6)

    for j in range(4):
        got = dot_nt(oh2[j * 256 : j * 256 + 256], z[...])
        out2[j * 256 : j * 256 + 256] = got[:, 0:128].astype(BF)
        rest = got[:, 128:160]
        for half in range(2):
            outb[j * 2 + half] = jnp.concatenate(
                [rest[(half * 8 + i) * 16 : (half * 8 + i) * 16 + 16] for i in range(NX)], axis=1
            ).astype(BF)
    for k in range(1, NY):
        to = mod(y + k, NY)
        go(remote(outb.at[to], inb.at[y], bsend.at[0, k], brecv.at[0, k], f, to * NX + xc))
    inb[y] = outb[y]

    @pl.loop(1, ND)
    def _(k):
        to = mod(d + k, ND)
        remote(
            out2.at[pl.ds(pl.multiple_of(to * 16, 16), 16)], in2.at[pl.ds(pl.multiple_of(d * 16, 16), 16)],
            asend, arecv, f, to,
        ).start()

    mine = pl.ds(pl.multiple_of(d * 16, 16), 16)
    in2[mine] = out2[mine]
    total = dot_nt(band[...], z[...])

    for k in range(1, NY):
        arrived(inb.at[mod(y + NY - k, NY)], brecv.at[0, k])
    for i in range(NX):
        outb2[i] = jnp.concatenate(
            [inb[r, :, i * 32 : i * 32 + 32].astype(F32) for r in range(NY)], axis=1
        ).astype(BF)
    for k in range(1, NX):
        to = mod(xc + k, NX)
        go(remote(outb2.at[to], inb2.at[xc], bsend.at[1, k], brecv.at[1, k], f, y * NX + to))
    inb2[xc] = outb2[xc]
    for k in range(1, NX):
        arrived(inb2.at[mod(xc + NX - k, NX)], brecv.at[1, k])
    flat = inb2[...].reshape(128, 256).astype(F32)
    flat = jnp.concatenate([flat[:, r * 32 : r * 32 + 32] for r in range(NY)], axis=0).astype(BF)
    few = dot(scat2[...], flat)
    total_b = total[:, 128:256] + jnp.concatenate([few, jnp.zeros((128, 96), F32)], axis=1)
    logits_ref[128:CLS, 0, :] = own_term[128:CLS] + (total_b.T)[0 : CLS - 128] / deg[0:1]

    arrived(in2.at[pl.ds(0, 1008)], arecv)
    total_a = total[:, 0:128] + dot(scat2[...], in2[...])
    logits_ref[0:128, 0, :] = own_term[0:128] + total_a.T / deg[0:1]

    arrived(out2.at[pl.ds(0, 1008)], asend)
    for k in range(1, NF):
        g = mod(f + k, NF)
        arrived(nsend_buf.at[g], nsend.at[g])
    for copy in sent:
        copy.wait_send()


def hand_over(hidden_ref, logits_ref, hidden_out, logits_out):
    hidden_out[...] = hidden_ref[...]
    logits_out[...] = logits_ref[...]


def on_device(
    features, tiles, tile_ids, sources, targets, counts, edge_weight, self_one, neigh_one, self_out, neigh_out
):
    vmem = pl.BlockSpec(memory_space=pltpu.VMEM)
    anywhere = pl.BlockSpec(memory_space=pl.ANY)
    dma = pltpu.SemaphoreType.DMA
    hidden, logits = pl.pallas_call(
        kernel,
        out_shape=(jax.ShapeDtypeStruct((128, HID), BF), jax.ShapeDtypeStruct((CLS, 1, 128), F32)),
        in_specs=[pl.BlockSpec(memory_space=pltpu.SMEM)] + [anywhere] * 10,
        out_specs=(vmem, vmem),
        scratch_shapes=[
            pltpu.VMEM((NF, 1, ND), I32),
            pltpu.VMEM((NF, 16, ND), I32),
            pltpu.VMEM((NF, 16, ND), I32),
            pltpu.VMEM((NF, 16, ND), BF),
            pltpu.VMEM((COLS, NODES), BF),
            pltpu.VMEM((CLS, HID), BF),
            pltpu.VMEM((CLS, HID), BF),
            pltpu.VMEM((36, 128, 128), BF),
            pltpu.VMEM((768, HID), BF),
            pltpu.VMEM((768, HID), BF),
            pltpu.VMEM((NY, COLS, NODES), BF),
            pltpu.VMEM((NY, 16, 128), I32),
            pltpu.VMEM((NY, 16, 128), I32),
            pltpu.VMEM((NY, COLS, NODES), BF),
            pltpu.VMEM((4, NX, COLS, 384), BF),
            pltpu.VMEM((4, NX, 80, 384), BF),
            pltpu.VMEM((80, NODES), BF),
            pltpu.VMEM((3, 512, 4096), BF),
            pltpu.VMEM((3, 32, 128), I32),
            pltpu.VMEM((3, 32, 128), F32),
            pltpu.VMEM((80, NODES), F32),
            pltpu.VMEM((NF, COLS, 128), BF),
            pltpu.VMEM((NF, COLS, 128), BF),
            pltpu.VMEM((NF, COLS, 128), BF),
            pltpu.VMEM((128, HID), F32),
            pltpu.VMEM((CPAD, HID), BF),
            pltpu.VMEM((CPAD, HID), BF),
            pltpu.VMEM((256, NODES), BF),
            pltpu.VMEM((1024, NODES), BF),
            pltpu.VMEM((128, 1024), BF),
            pltpu.VMEM((1024, 128), BF),
            pltpu.VMEM((1024, 128), BF),
            pltpu.VMEM((8, 128), F32),
            pltpu.VMEM((36, 80, 128), F32),
            pltpu.VMEM((128, NODES), BF),
            pltpu.VMEM((NY, 16, 256), BF),
            pltpu.VMEM((NY, 16, 256), BF),
            pltpu.VMEM((NY, 16, 256), BF),
            pltpu.VMEM((NY, 16, 256), BF),
            dma((10,)),
            dma((NY, 2)), dma((NY, 2)),
            dma((NY,)), dma((NY,)),
            dma((NF,)), dma((NF,)),
            dma((6, NX)), dma((6, NX)),
            dma((NF,)), dma((NF,)),
            dma((2, 7)), dma((2, 7)),
            dma, dma,
            dma((2, 8)), dma((2, 8)),
        ],
        compiler_params=pltpu.CompilerParams(
            collective_id=0, has_side_effects=True, vmem_limit_bytes=56 * 1024 * 1024
        ),
    )(
        tile_ids[0].T,
        jnp.transpose(counts, (2, 0, 1)),
        jnp.transpose(sources[0], (1, 2, 0)),
        jnp.transpose(targets[0], (1, 2, 0)),
        jnp.transpose(edge_weight[0], (1, 2, 0)),
        features[0].T,
        tiles[0],
        self_one,
        neigh_one,
        self_out.T,
        neigh_out.T,
    )
    hidden, logits = pl.pallas_call(
        hand_over,
        out_shape=(jax.ShapeDtypeStruct((128, HID), BF), jax.ShapeDtypeStruct((CLS, 1, 128), F32)),
        in_specs=[vmem] * 2,
        out_specs=(vmem, vmem),
    )(hidden, logits)
    return hidden[None], jnp.transpose(logits, (1, 0, 2))


def solution(mesh):
    placed = (
        P("dom", None, "feat"),
        P("dom", None, None, None),
        P("dom", None, None),
        P("dom", None, None, None),
        P("dom", None, None, None),
        P("dom", None, None),
        P("dom", None, None, None),
        P(),
        P(),
        P(),
        P(),
    )
    return jax.shard_map(
        on_device,
        mesh=mesh,
        in_specs=placed,
        out_specs=(P("dom", "feat", None), P("dom", None, "feat")),
        check_vma=False,
    )
```

```python
import jax
import jax.numpy as jnp
from jax import lax
from jax.experimental import pallas as pl
from jax.experimental.pallas import tpu as pltpu
from jax.sharding import PartitionSpec as P

MESH = pl.DeviceIdType.MESH
BF = jnp.bfloat16
F32 = jnp.float32
I32 = jnp.int32
I16 = jnp.int16
NT = (((1,), (1,)), ((), ()))

NF = 12
ND = 64
NY = 8
NX = 8
COLS = 64
NODES = 1536
HID = 1024
CLS = 153
CPAD = 160
PAIRS = ((0, 1), (2, 7), (6, 3), (4, 5))


def iota(shape, dim):
    return lax.broadcasted_iota(I32, shape, dim)


def mod(a, n):
    return lax.rem(a, jnp.int32(n))


def dot(a, b):
    return jnp.dot(a, b, preferred_element_type=F32)


def dot_nt(a, b):
    return lax.dot_general(a, b, NT, preferred_element_type=F32)


def kernel(
    ids, counts_hbm, sources_hbm, targets_hbm, weights_hbm, feat_hbm, tiles_hbm, s1_hbm, n1_hbm, so_hbm, no_hbm,
    hidden_ref, logits_ref,
    counts, sources, targets, weights, feat, so, no, tiles, s1, n1, tab, idx_out, idx_in, picked, out1, in1, ftd, scat, rows_t, rows_w, acc,
    frows, nsend_buf, nrows, pre, wso, wno, z, oh2, scat2, out2, in2, deg, prod, band, outb, inb, outb2, inb2,
    loc, tsend, trecv, isend, irecv, fsend, frecv, xsend, xrecv, nsend, nrecv, zsend, zrecv, asend, arecv, bsend, brecv,
):
    f = lax.axis_index("feat")
    d = lax.axis_index("dom")
    y = lax.div(d, jnp.int32(NX))
    xc = mod(d, NX)
    core = mod(d, 2)

    def remote(src, dst, ss, rs, fi, di):
        return pltpu.make_async_remote_copy(
            src_ref=src, dst_ref=dst, send_sem=ss, recv_sem=rs, device_id=(fi, di), device_id_type=MESH
        )

    def arrived(dst, rs):
        pltpu.make_async_copy(dst, dst, rs).wait()

    def row_peer(k):
        return mod(y + k, NY) * NX + xc

    def col_peer(k):
        return y * NX + mod(xc + k, NX)

    barrier = pltpu.get_barrier_semaphore()
    for k in range(1, NY):
        pl.semaphore_signal(barrier, inc=1, device_id=(f, row_peer(k)), device_id_type=MESH)
    for k in range(1, NX):
        pl.semaphore_signal(barrier, inc=1, device_id=(f, col_peer(k)), device_id_type=MESH)
    for k in range(1, NF):
        pl.semaphore_signal(barrier, inc=1, device_id=(mod(f + k, NF), d), device_id_type=MESH)

    loads = [
        pltpu.make_async_copy(far, near, loc.at[i])
        for i, (far, near) in enumerate((
            (sources_hbm, sources), (feat_hbm, feat), (targets_hbm, targets), (counts_hbm, counts),
            (weights_hbm, weights), (tiles_hbm, tiles), (s1_hbm, s1), (n1_hbm, n1), (no_hbm, no), (so_hbm, so),
        ))
    ]
    for load in loads:
        load.start()

    spread_out = [place * 3 + third for third in range(3) for place in range(4)]

    loads[0].wait()
    src = jnp.concatenate([sources[g] for g in spread_out], axis=0)
    both = jnp.concatenate([src >> 8, src & 255], axis=0).astype(F32).astype(BF)
    r32 = iota((32, ND), 0)
    e32 = iota((32, ND), 1)
    flip = (lax.div(r32, 4) + y) & 1
    halves = []
    for h in range(2):
        pick = (e32 == r32 * 2 + (flip ^ h)).astype(F32).astype(BF)
        got = dot_nt(pick, both)
        halves.append((got[:, :192] * 256.0 + got[:, 192:]).astype(I32))
    thirds = [
        jnp.concatenate([halves[0][:, q * 64 : q * 64 + 64], halves[1][:, q * 64 : q * 64 + 64]], axis=1)
        for q in range(3)
    ]
    for row in range(NY):
        some = [third[row * 4 : row * 4 + 4] for third in thirds] + [jnp.zeros((4, 128), I32)]
        idx_out[row] = jnp.concatenate(some, axis=0).astype(I16)
    idx_in[0] = idx_out[y]

    loads[1].wait()
    pl.semaphore_wait(barrier, NY - 1 + NX - 1 + NF - 1)

    sent = []

    def go(copy):
        copy.start()
        sent.append(copy)

    def table(slot):
        return feat if slot == 0 else tab.at[slot]

    def pass_on(from_slot, to_slot, half, di):
        part = pl.ds(half * 32, 32)
        go(remote(
            table(from_slot).at[part], tab.at[to_slot, part],
            tsend.at[to_slot, half], trecv.at[to_slot, half], f, di,
        ))

    def took(slot, half):
        arrived(tab.at[slot, pl.ds(half * 32, 32)], trecv.at[slot, half])

    up = row_peer(1)
    down = row_peer(NY - 1)
    for half in range(2):
        pass_on(0, 1, half, up)
        pass_on(0, 7, half, down)
    for k in range(1, NY):
        to = mod(y + k, NY)
        go(remote(idx_out.at[to], idx_in.at[k], isend.at[k], irecv.at[k], f, to * NX + xc))
    for k in range(1, NF):
        g = mod(f + k, NF)
        go(remote(
            feat.at[:, pl.ds(pl.multiple_of(g * 128, 128), 128)], frows.at[f], fsend.at[k], frecv.at[k], g, d
        ))
    frows[f] = feat[:, pl.ds(pl.multiple_of(f * 128, 128), 128)]

    def gather(slot, half):
        here = table(slot)
        rows = slice(half * 32, half * 32 + 32)
        ids_here = idx_in[slot].astype(I32)
        for r in range(6):
            wide = jnp.concatenate([here[rows, k * 256 : k * 256 + 256] for k in range(6)], axis=0)
            pick = jnp.concatenate([ids_here[2 * r : 2 * r + 1], ids_here[2 * r + 1 : 2 * r + 2]], axis=1)
            low = pick & 255
            high = pick >> 8
            one_hot = (iota((256, 256), 0) == low).astype(F32).astype(BF)
            got = dot(wide, one_hot)
            kept = jnp.zeros((32, 256), F32)
            for k in range(6):
                kept = jnp.where(high == k, got[k * 32 : k * 32 + 32], kept)
            picked[slot, rows, r * 256 : r * 256 + 256] = kept.astype(BF)

    first_half = iota((COLS, 128), 1) < 64

    def merge(b, q):
        even, odd = PAIRS[b]
        for col in range(4):
            at = (q * 4 + col) * 128
            one = picked[even, :, at : at + 128]
            two = picked[odd, :, at : at + 128]
            out1[b, 2 * col, :, q * 128 : q * 128 + 128] = jnp.where(first_half, one, two)
            out1[b, 2 * col + 1, :, q * 128 : q * 128 + 128] = jnp.where(first_half, two, one)

    def merge_and_send(b, half):
        even, odd = PAIRS[b]
        rows = slice(half * 32, half * 32 + 32)
        for q in range(3):
            for col in range(4):
                at = (q * 4 + col) * 128
                one = picked[even, rows, at : at + 128]
                two = picked[odd, rows, at : at + 128]
                out1[b, 2 * col, rows, q * 128 : q * 128 + 128] = jnp.where(first_half[rows], one, two)
                out1[b, 2 * col + 1, rows, q * 128 : q * 128 + 128] = jnp.where(first_half[rows], two, one)
        part = pl.ds(half * 32, 32)
        for k in (4, 3, 5, 2, 6, 1, 7):
            to = mod(xc + k, NX)
            go(remote(
                out1.at[b, to, part], in1.at[b, xc, part],
                xsend.at[b * 2 + half, k], xrecv.at[b * 2 + half, k], f, y * NX + to,
            ))
        in1[b, xc, rows] = out1[b, xc, rows]

    def last_batch(q):
        merge(3, q)
        part = pl.ds(q * 128, 128)
        for k in (4, 3, 5, 2, 6, 1, 7):
            to = mod(xc + k, NX)
            go(remote(
                out1.at[3, to, :, part], in1.at[3, xc, pl.ds(0, COLS), part],
                xsend.at[6 + q, k], xrecv.at[6 + q, k], f, y * NX + to,
            ))
        in1[3, xc, 0:COLS, part] = out1[3, xc, :, part]

    gather(0, 0)
    gather(0, 1)

    for i in (2, 3, 4):
        loads[i].wait()
    t_all = jnp.concatenate(
        [jnp.where(iota((16, ND), 0) < counts[g], targets[g], -512) for g in spread_out], axis=0
    )
    w_all = jnp.concatenate([weights[g] for g in spread_out], axis=0)
    both = jnp.concatenate([t_all.astype(F32).astype(BF), w_all], axis=0)
    batch = lax.div(r32, 8)
    halves = []
    for h in range(2):
        par = core ^ h
        far = jnp.zeros((32, ND), I32)
        for b in range(4):
            dist = jnp.where(par == 0, PAIRS[b][0], PAIRS[b][1])
            far = jnp.where(batch == b, dist, far)
        origin = ((y + 8 - far) & 7) * 8 + (r32 & 7)
        halves.append(dot_nt((e32 == origin).astype(F32).astype(BF), both))
    for q in range(3):
        lanes = iota((32, 128), 1)
        base = (lax.div(lanes, 16) & 3) * 128
        t_tile = jnp.concatenate([halves[0][:, q * 64 : q * 64 + 64], halves[1][:, q * 64 : q * 64 + 64]], axis=1)
        w_tile = jnp.concatenate(
            [halves[0][:, 192 + q * 64 : 256 + q * 64], halves[1][:, 192 + q * 64 : 256 + q * 64]], axis=1
        )
        rows_t[q] = t_tile.astype(I32) + base
        rows_w[q] = w_tile

    def build(b):
        @pl.loop(0, 8)
        def _(i):
            r = b * 8 + i
            for q in range(3):
                t = rows_t[q, pl.ds(r, 1), :]
                w = rows_w[q, pl.ds(r, 1), :]
                scat[q, :, pl.ds(pl.multiple_of(r * 128, 128), 128)] = jnp.where(
                    iota((512, 128), 0) == t, w, 0.0
                ).astype(BF)

    def scatter_part(b, q):
        rows = jnp.concatenate([in1[b, i, :, q * 128 : q * 128 + 128] for i in range(NX)], axis=1)
        acc[:, q * 512 : q * 512 + 512] += dot_nt(rows, scat[q, :, b * 1024 : b * 1024 + 1024])

    def arrive_batch(b):
        for k in range(1, NX):
            for half in range(2):
                arrived(in1.at[b, mod(xc + NX - k, NX), pl.ds(half * 32, 32)], xrecv.at[b * 2 + half, k])

    def scatter(b):
        arrive_batch(b)
        for q in range(3):
            scatter_part(b, q)

    def multiply(low, high):
        @pl.loop(low, high)
        def _(r):
            for i in range(6):
                t = r * 6 + i
                cols = jnp.zeros((80, 128), BF)
                for q in range(NF):
                    cols = jnp.where(ids[1, t] == q, ftd[:, q * 128 : q * 128 + 128], cols)
                prod[t] = dot_nt(cols, tiles[t])

    build(0)
    build(1)
    in1[:, :, COLS:80, :] = jnp.ones((4, NX, 16, 384), BF)
    z[CPAD:256] = jnp.zeros((256 - CPAD, NODES), BF)
    ftd[0:COLS] = feat[...]
    ftd[COLS:80] = jnp.ones((16, NODES), BF)

    took(1, 0)
    pass_on(1, 2, 0, up)
    took(7, 0)
    pass_on(7, 6, 0, down)
    arrived(idx_in.at[1], irecv.at[1])
    gather(1, 0)
    merge_and_send(0, 0)
    took(1, 1)
    pass_on(1, 2, 1, up)
    took(7, 1)
    pass_on(7, 6, 1, down)
    gather(1, 1)
    merge_and_send(0, 1)
    arrived(idx_in.at[7], irecv.at[7])
    gather(7, 0)
    loads[5].wait()
    multiply(0, 3)

    took(2, 0)
    pass_on(2, 3, 0, up)
    took(6, 0)
    pass_on(6, 5, 0, down)
    arrived(idx_in.at[2], irecv.at[2])
    gather(2, 0)
    merge_and_send(1, 0)
    gather(7, 1)
    took(2, 1)
    pass_on(2, 3, 1, up)
    took(6, 1)
    pass_on(6, 5, 1, down)
    gather(2, 1)
    merge_and_send(1, 1)
    build(2)
    arrived(idx_in.at[6], irecv.at[6])
    gather(6, 0)

    took(3, 0)
    pass_on(3, 4, 0, up)
    took(5, 0)
    arrived(idx_in.at[3], irecv.at[3])
    gather(3, 0)
    merge_and_send(2, 0)
    gather(6, 1)
    took(3, 1)
    took(5, 1)
    pass_on(5, 4, 1, down)
    gather(3, 1)
    merge_and_send(2, 1)
    arrived(idx_in.at[5], irecv.at[5])
    gather(5, 0)
    gather(5, 1)
    build(3)
    multiply(3, 6)
    took(4, 0)
    arrived(idx_in.at[4], irecv.at[4])
    gather(4, 0)
    took(4, 1)
    gather(4, 1)
    for q in range(3):
        last_batch(q)

    @pl.loop(0, NF)
    def _(p):
        r = mod(p, 4) * 3 + lax.div(p, 4)
        total = jnp.zeros((80, 128), F32)
        for t in range(36):
            total = total + jnp.where(ids[0, t] == r, prod[t], 0.0)
        acc[:, pl.ds(pl.multiple_of(p * 128, 128), 128)] = total

    scatter(0)
    scatter(1)
    scatter(2)
    loads[6].wait()
    for k in range(1, NF):
        arrived(frows.at[mod(f + NF - k, NF)], frecv.at[k])
    pre[...] = dot(frows[...].reshape(768, 128).T, s1[...])
    for q in range(3):
        for k in range(1, NX):
            arrived(in1.at[3, mod(xc + NX - k, NX), pl.ds(0, COLS), pl.ds(q * 128, 128)], xrecv.at[6 + q, k])
        scatter_part(3, q)
        for i in range(4):
            place = mod(lax.div(f, 3) + i, 4)
            g = place * 3 + q
            part = acc[:, pl.ds(pl.multiple_of(q * 512 + place * 128, 128), 128)]
            nsend_buf[g] = (part[0:COLS] / part[COLS : COLS + 1]).astype(BF)

            @pl.when(f != g)
            def _():
                remote(nsend_buf.at[g], nrows.at[f], nsend.at[g], nrecv.at[f], g, d).start()

    nrows[f] = nsend_buf[f]
    deg[...] = acc[COLS : COLS + 8, pl.ds(pl.multiple_of(mod(f, 3) * 512 + lax.div(f, 3) * 128, 128), 128)]
    loads[7].wait()
    loads[8].wait()
    wno[CLS - 9 : CPAD] = jnp.zeros((16, HID), BF)
    wno[0:CLS] = no[...]
    s2 = sources[f]
    high2 = (s2 >> 8).astype(F32).astype(BF)
    low2 = (s2 & 255).astype(F32).astype(BF)

    @pl.loop(0, 8)
    def _(j):
        rows = iota((128, ND), 0) + j * 128
        expand = (lax.div(rows, 16) == iota((128, ND), 1)).astype(F32).astype(BF)
        value = dot_nt(expand, high2) * 256.0 + dot_nt(expand, low2)
        mine = (iota((128, 16), 0) & 15) == iota((128, 16), 1)
        node = jnp.sum(jnp.where(mine, value, 0.0), axis=1, keepdims=True).astype(I32)
        for q in range(NF):
            oh2[pl.ds(pl.multiple_of(j * 128, 128), 128), q * 128 : q * 128 + 128] = (
                (iota((128, 128), 1) + q * 128) == node
            ).astype(F32).astype(BF)

    for k in range(1, NF):
        g = mod(f + NF - k, NF)
        arrived(nrows.at[g], nrecv.at[g])

    hidden = jnp.maximum(pre[...] + dot(nrows[...].reshape(768, 128).T, n1[...]), 0.0).astype(BF)
    hidden_ref[...] = hidden

    def block_at(g):
        return z.at[pl.ds(0, CPAD), pl.ds(pl.multiple_of(g * 128, 128), 128)]

    z[0:CPAD, pl.ds(pl.multiple_of(f * 128, 128), 128)] = dot_nt(wno[...], hidden_ref[...]).astype(BF)

    way = 1 - 2 * core
    ways = (way, -way)

    def from_far(side, k):
        return block_at(mod(f + NF - ways[side] * k, NF))

    def throw(side, held, hops):
        block = from_far(side, held)
        k = held + hops
        go(remote(block, block, zsend.at[side, k], zrecv.at[side, k], mod(f + NF + ways[side] * hops, NF), d))

    def caught(side, k):
        arrived(from_far(side, k), zrecv.at[side, k])

    for hops in (4, 2, 1):
        for side in range(2):
            throw(side, 0, hops)
    caught(0, 4)
    throw(0, 4, 2)
    throw(0, 4, 1)
    caught(1, 4)
    throw(1, 4, 1)
    for side in range(2):
        caught(side, 2)
        throw(side, 2, 1)

    loads[9].wait()
    wso[CLS - 9 : CPAD] = jnp.zeros((16, HID), BF)
    wso[0:CLS] = so[...]
    own_term = dot_nt(wso[...], hidden_ref[...])
    lane = iota((ND, 1024), 1)
    spread = (lax.div(lane, 16) == iota((ND, 1024), 0)).astype(F32).astype(BF)
    t2 = jnp.where(iota((16, ND), 0) < counts[f], targets[f], -512).astype(F32).astype(BF)
    own = iota((16, 1024), 0) == (iota((16, 1024), 1) & 15)
    t_row = jnp.sum(jnp.where(own, dot(t2, spread), 0.0), axis=0, keepdims=True).astype(I32)
    w_row = jnp.sum(jnp.where(own, dot(weights[f], spread), 0.0), axis=0, keepdims=True)
    scat2[...] = jnp.where(iota((128, 1024), 0) == t_row, w_row, 0.0).astype(BF)

    @pl.loop(0, NF)
    def _(q):
        block = jnp.zeros((128, 128), BF)
        for t in range(36):
            block = jnp.where((ids[0, t] == f) & (ids[1, t] == q), tiles[t], block)
        band[:, pl.ds(pl.multiple_of(q * 128, 128), 128)] = block

    for k in (1, 3, 5):
        caught(0, k)
        caught(1, k)
    caught(0, 6)

    def quarter(j):
        base = mod(lax.div(d, 16) + j, 4) * 16
        rows = pl.ds(pl.multiple_of(base * 16, 256), 256)
        got = dot_nt(oh2[rows], z[...])
        out2[rows] = got[:, 0:128].astype(BF)
        rest = got[:, 128:160]
        for half in range(2):
            outb[lax.div(base, 8) + half] = jnp.concatenate(
                [rest[(half * 8 + i) * 16 : (half * 8 + i) * 16 + 16] for i in range(NX)], axis=1
            ).astype(BF)

    def straight(j):
        base = mod(lax.div(d, 16) + j, 4) * 16

        @pl.loop(0, 16)
        def _(k):
            to = base + mod(d + k, 16)

            @pl.when(to != d)
            def _():
                remote(
                    out2.at[pl.ds(pl.multiple_of(to * 16, 16), 16)], in2.at[pl.ds(pl.multiple_of(d * 16, 16), 16)],
                    asend, arecv, f, to,
                ).start()

    quarter(2)
    straight(2)
    for j in (0, 1, 3):
        quarter(j)
    for k in range(1, NY):
        to = mod(y + k, NY)
        go(remote(outb.at[to], inb.at[y], bsend.at[0, k], brecv.at[0, k], f, to * NX + xc))
    inb[y] = outb[y]
    for j in (1, 3, 0):
        straight(j)

    mine = pl.ds(pl.multiple_of(d * 16, 16), 16)
    in2[mine] = out2[mine]
    total = dot_nt(band[...], z[...])

    for k in range(1, NY):
        arrived(inb.at[mod(y + NY - k, NY)], brecv.at[0, k])
    for i in range(NX):
        outb2[i] = jnp.concatenate(
            [inb[r, :, i * 32 : i * 32 + 32].astype(F32) for r in range(NY)], axis=1
        ).astype(BF)
    for k in range(1, NX):
        to = mod(xc + k, NX)
        go(remote(outb2.at[to], inb2.at[xc], bsend.at[1, k], brecv.at[1, k], f, y * NX + to))
    inb2[xc] = outb2[xc]
    for k in range(1, NX):
        arrived(inb2.at[mod(xc + NX - k, NX)], brecv.at[1, k])
    flat = inb2[...].reshape(128, 256).astype(F32)
    flat = jnp.concatenate([flat[:, r * 32 : r * 32 + 32] for r in range(NY)], axis=0).astype(BF)
    few = dot(scat2[...], flat)
    total_b = total[:, 128:256] + jnp.concatenate([few, jnp.zeros((128, 96), F32)], axis=1)
    logits_ref[128:CLS, 0, :] = own_term[128:CLS] + (total_b.T)[0 : CLS - 128] / deg[0:1]

    arrived(in2.at[pl.ds(0, 1008)], arecv)
    total_a = total[:, 0:128] + dot(scat2[...], in2[...])
    logits_ref[0:128, 0, :] = own_term[0:128] + total_a.T / deg[0:1]

    arrived(out2.at[pl.ds(0, 1008)], asend)
    for k in range(1, NF):
        g = mod(f + k, NF)
        arrived(nsend_buf.at[g], nsend.at[g])
    for copy in sent:
        copy.wait_send()


def hand_over(hidden_ref, logits_ref, hidden_out, logits_out):
    hidden_out[...] = hidden_ref[...]
    logits_out[...] = logits_ref[...]


def on_device(
    features, tiles, tile_ids, sources, targets, counts, edge_weight, self_one, neigh_one, self_out, neigh_out
):
    vmem = pl.BlockSpec(memory_space=pltpu.VMEM)
    anywhere = pl.BlockSpec(memory_space=pl.ANY)
    dma = pltpu.SemaphoreType.DMA
    hidden, logits = pl.pallas_call(
        kernel,
        out_shape=(jax.ShapeDtypeStruct((128, HID), BF), jax.ShapeDtypeStruct((CLS, 1, 128), F32)),
        in_specs=[pl.BlockSpec(memory_space=pltpu.SMEM)] + [anywhere] * 10,
        out_specs=(vmem, vmem),
        scratch_shapes=[
            pltpu.VMEM((NF, 1, ND), I32),
            pltpu.VMEM((NF, 16, ND), I32),
            pltpu.VMEM((NF, 16, ND), I32),
            pltpu.VMEM((NF, 16, ND), BF),
            pltpu.VMEM((COLS, NODES), BF),
            pltpu.VMEM((CLS, HID), BF),
            pltpu.VMEM((CLS, HID), BF),
            pltpu.VMEM((36, 128, 128), BF),
            pltpu.VMEM((768, HID), BF),
            pltpu.VMEM((768, HID), BF),
            pltpu.VMEM((NY, COLS, NODES), BF),
            pltpu.VMEM((NY, 16, 128), I16),
            pltpu.VMEM((NY, 16, 128), I16),
            pltpu.VMEM((NY, COLS, NODES), BF),
            pltpu.VMEM((4, NX, COLS, 384), BF),
            pltpu.VMEM((4, NX, 80, 384), BF),
            pltpu.VMEM((80, NODES), BF),
            pltpu.VMEM((3, 512, 4096), BF),
            pltpu.VMEM((3, 32, 128), I32),
            pltpu.VMEM((3, 32, 128), F32),
            pltpu.VMEM((80, NODES), F32),
            pltpu.VMEM((NF, COLS, 128), BF),
            pltpu.VMEM((NF, COLS, 128), BF),
            pltpu.VMEM((NF, COLS, 128), BF),
            pltpu.VMEM((128, HID), F32),
            pltpu.VMEM((CPAD, HID), BF),
            pltpu.VMEM((CPAD, HID), BF),
            pltpu.VMEM((256, NODES), BF),
            pltpu.VMEM((1024, NODES), BF),
            pltpu.VMEM((128, 1024), BF),
            pltpu.VMEM((1024, 128), BF),
            pltpu.VMEM((1024, 128), BF),
            pltpu.VMEM((8, 128), F32),
            pltpu.VMEM((36, 80, 128), F32),
            pltpu.VMEM((128, NODES), BF),
            pltpu.VMEM((NY, 16, 256), BF),
            pltpu.VMEM((NY, 16, 256), BF),
            pltpu.VMEM((NY, 16, 256), BF),
            pltpu.VMEM((NY, 16, 256), BF),
            dma((10,)),
            dma((NY, 2)), dma((NY, 2)),
            dma((NY,)), dma((NY,)),
            dma((NF,)), dma((NF,)),
            dma((9, NX)), dma((9, NX)),
            dma((NF,)), dma((NF,)),
            dma((2, 7)), dma((2, 7)),
            dma, dma,
            dma((2, 8)), dma((2, 8)),
        ],
        compiler_params=pltpu.CompilerParams(
            collective_id=0, has_side_effects=True, vmem_limit_bytes=56 * 1024 * 1024
        ),
    )(
        tile_ids[0].T,
        jnp.transpose(counts, (2, 0, 1)),
        jnp.transpose(sources[0], (1, 2, 0)),
        jnp.transpose(targets[0], (1, 2, 0)),
        jnp.transpose(edge_weight[0], (1, 2, 0)),
        features[0].T,
        tiles[0],
        self_one,
        neigh_one,
        self_out.T,
        neigh_out.T,
    )
    hidden, logits = pl.pallas_call(
        hand_over,
        out_shape=(jax.ShapeDtypeStruct((128, HID), BF), jax.ShapeDtypeStruct((CLS, 1, 128), F32)),
        in_specs=[vmem] * 2,
        out_specs=(vmem, vmem),
    )(hidden, logits)
    return hidden[None], jnp.transpose(logits, (1, 0, 2))


def solution(mesh):
    placed = (
        P("dom", None, "feat"),
        P("dom", None, None, None),
        P("dom", None, None),
        P("dom", None, None, None),
        P("dom", None, None, None),
        P("dom", None, None),
        P("dom", None, None, None),
        P(),
        P(),
        P(),
        P(),
    )
    return jax.shard_map(
        on_device,
        mesh=mesh,
        in_specs=placed,
        out_specs=(P("dom", "feat", None), P("dom", None, "feat")),
        check_vma=False,
    )
```

```python
import jax
import jax.numpy as jnp
from jax import lax
from jax.experimental import pallas as pl
from jax.experimental.pallas import tpu as pltpu
from jax.sharding import PartitionSpec as P

MESH = pl.DeviceIdType.MESH
BF = jnp.bfloat16
F32 = jnp.float32
I32 = jnp.int32
I16 = jnp.int16
NT = (((1,), (1,)), ((), ()))

NF = 12
ND = 64
NY = 8
NX = 8
COLS = 64
NODES = 1536
HID = 1024
CLS = 153
CPAD = 160
PAIRS = ((0, 1), (2, 7), (6, 3), (4, 5))


def iota(shape, dim):
    return lax.broadcasted_iota(I32, shape, dim)


def mod(a, n):
    return lax.rem(a, jnp.int32(n))


def dot(a, b):
    return jnp.dot(a, b, preferred_element_type=F32)


def dot_nt(a, b):
    return lax.dot_general(a, b, NT, preferred_element_type=F32)


def kernel(
    ids, counts_hbm, sources_hbm, targets_hbm, weights_hbm, feat_hbm, tiles_hbm, s1_hbm, n1_hbm, so_hbm, no_hbm,
    hidden_ref, logits_ref,
    counts, sources, targets, weights, feat, so, no, tiles, s1, n1, tab, idx_out, idx_in, picked, out1, in1, ftd, scat, rows_t, rows_w, acc,
    frows, nsend_buf, nrows, pre, wso, wno, z, oh2, scat2, out2, in2, deg, prod, band, outb, inb, outb2, inb2,
    loc, tsend, trecv, isend, irecv, fsend, frecv, xsend, xrecv, nsend, nrecv, zsend, zrecv, asend, arecv, bsend, brecv,
):
    f = lax.axis_index("feat")
    d = lax.axis_index("dom")
    y = lax.div(d, jnp.int32(NX))
    xc = mod(d, NX)
    core = mod(d, 2)

    def remote(src, dst, ss, rs, fi, di):
        return pltpu.make_async_remote_copy(
            src_ref=src, dst_ref=dst, send_sem=ss, recv_sem=rs, device_id=(fi, di), device_id_type=MESH
        )

    def arrived(dst, rs):
        pltpu.make_async_copy(dst, dst, rs).wait()

    def row_peer(k):
        return mod(y + k, NY) * NX + xc

    def col_peer(k):
        return y * NX + mod(xc + k, NX)

    barrier = pltpu.get_barrier_semaphore()
    for k in range(1, NY):
        pl.semaphore_signal(barrier, inc=1, device_id=(f, row_peer(k)), device_id_type=MESH)
    for k in range(1, NX):
        pl.semaphore_signal(barrier, inc=1, device_id=(f, col_peer(k)), device_id_type=MESH)
    for k in range(1, NF):
        pl.semaphore_signal(barrier, inc=1, device_id=(mod(f + k, NF), d), device_id_type=MESH)

    loads = [
        pltpu.make_async_copy(far, near, loc.at[i])
        for i, (far, near) in enumerate((
            (sources_hbm, sources), (feat_hbm, feat), (targets_hbm, targets), (counts_hbm, counts),
            (weights_hbm, weights), (tiles_hbm, tiles), (s1_hbm, s1), (n1_hbm, n1), (no_hbm, no), (so_hbm, so),
        ))
    ]
    for load in loads:
        load.start()

    pl.semaphore_wait(barrier, NY - 1 + NX - 1 + NF - 1)

    sent = []

    def go(copy):
        copy.start()
        sent.append(copy)

    def table(slot):
        return feat if slot == 0 else tab.at[slot]

    def travels(slot):
        return feat_hbm if slot == 0 else tab.at[slot]

    def pass_on(from_slot, to_slot, half, di):
        part = pl.ds(half * 32, 32)
        go(remote(
            travels(from_slot).at[part], tab.at[to_slot, part],
            tsend.at[to_slot, half], trecv.at[to_slot, half], f, di,
        ))

    def took(slot, half):
        arrived(tab.at[slot, pl.ds(half * 32, 32)], trecv.at[slot, half])

    up = row_peer(1)
    down = row_peer(NY - 1)
    for half in range(2):
        pass_on(0, 1, half, up)
        pass_on(0, 7, half, down)
    spread_out = [place * 3 + third for third in range(3) for place in range(4)]

    loads[0].wait()
    src = jnp.concatenate([sources[g] for g in spread_out], axis=0)
    both = jnp.concatenate([src >> 8, src & 255], axis=0).astype(F32).astype(BF)
    r32 = iota((32, ND), 0)
    e32 = iota((32, ND), 1)
    flip = (lax.div(r32, 4) + y) & 1
    halves = []
    for h in range(2):
        pick = (e32 == r32 * 2 + (flip ^ h)).astype(F32).astype(BF)
        got = dot_nt(pick, both)
        halves.append((got[:, :192] * 256.0 + got[:, 192:]).astype(I32))
    thirds = [
        jnp.concatenate([halves[0][:, q * 64 : q * 64 + 64], halves[1][:, q * 64 : q * 64 + 64]], axis=1)
        for q in range(3)
    ]
    for row in range(NY):
        some = [third[row * 4 : row * 4 + 4] for third in thirds] + [jnp.zeros((4, 128), I32)]
        idx_out[row] = jnp.concatenate(some, axis=0).astype(I16)
    idx_in[0] = idx_out[y]

    for k in range(1, NY):
        to = mod(y + k, NY)
        go(remote(idx_out.at[to], idx_in.at[k], isend.at[k], irecv.at[k], f, to * NX + xc))
    for k in range(1, NF):
        g = mod(f + k, NF)
        go(remote(
            feat_hbm.at[:, pl.ds(pl.multiple_of(g * 128, 128), 128)], frows.at[f], fsend.at[k], frecv.at[k], g, d
        ))
    loads[1].wait()
    frows[f] = feat[:, pl.ds(pl.multiple_of(f * 128, 128), 128)]

    def gather(slot, half):
        here = table(slot)
        rows = slice(half * 32, half * 32 + 32)
        ids_here = idx_in[slot].astype(I32)
        for r in range(6):
            wide = jnp.concatenate([here[rows, k * 256 : k * 256 + 256] for k in range(6)], axis=0)
            pick = jnp.concatenate([ids_here[2 * r : 2 * r + 1], ids_here[2 * r + 1 : 2 * r + 2]], axis=1)
            low = pick & 255
            high = pick >> 8
            one_hot = (iota((256, 256), 0) == low).astype(F32).astype(BF)
            got = dot(wide, one_hot)
            kept = jnp.zeros((32, 256), F32)
            for k in range(6):
                kept = jnp.where(high == k, got[k * 32 : k * 32 + 32], kept)
            picked[slot, rows, r * 256 : r * 256 + 256] = kept.astype(BF)

    first_half = iota((COLS, 128), 1) < 64

    def merge(b, q):
        even, odd = PAIRS[b]
        for col in range(4):
            at = (q * 4 + col) * 128
            one = picked[even, :, at : at + 128]
            two = picked[odd, :, at : at + 128]
            out1[b, 2 * col, :, q * 128 : q * 128 + 128] = jnp.where(first_half, one, two)
            out1[b, 2 * col + 1, :, q * 128 : q * 128 + 128] = jnp.where(first_half, two, one)

    def merge_and_send(b, half):
        even, odd = PAIRS[b]
        rows = slice(half * 32, half * 32 + 32)
        for q in range(3):
            for col in range(4):
                at = (q * 4 + col) * 128
                one = picked[even, rows, at : at + 128]
                two = picked[odd, rows, at : at + 128]
                out1[b, 2 * col, rows, q * 128 : q * 128 + 128] = jnp.where(first_half[rows], one, two)
                out1[b, 2 * col + 1, rows, q * 128 : q * 128 + 128] = jnp.where(first_half[rows], two, one)
        part = pl.ds(half * 32, 32)
        for k in (4, 3, 5, 2, 6, 1, 7):
            to = mod(xc + k, NX)
            go(remote(
                out1.at[b, to, part], in1.at[b, xc, part],
                xsend.at[b * 2 + half, k], xrecv.at[b * 2 + half, k], f, y * NX + to,
            ))
        in1[b, xc, rows] = out1[b, xc, rows]

    def last_batch(q):
        merge(3, q)
        part = pl.ds(q * 128, 128)
        for k in (4, 3, 5, 2, 6, 1, 7):
            to = mod(xc + k, NX)
            go(remote(
                out1.at[3, to, :, part], in1.at[3, xc, pl.ds(0, COLS), part],
                xsend.at[6 + q, k], xrecv.at[6 + q, k], f, y * NX + to,
            ))
        in1[3, xc, 0:COLS, part] = out1[3, xc, :, part]

    gather(0, 0)
    gather(0, 1)

    for i in (2, 3, 4):
        loads[i].wait()
    t_all = jnp.concatenate(
        [jnp.where(iota((16, ND), 0) < counts[g], targets[g], -512) for g in spread_out], axis=0
    )
    w_all = jnp.concatenate([weights[g] for g in spread_out], axis=0)
    both = jnp.concatenate([t_all.astype(F32).astype(BF), w_all], axis=0)
    batch = lax.div(r32, 8)
    halves = []
    for h in range(2):
        par = core ^ h
        far = jnp.zeros((32, ND), I32)
        for b in range(4):
            dist = jnp.where(par == 0, PAIRS[b][0], PAIRS[b][1])
            far = jnp.where(batch == b, dist, far)
        origin = ((y + 8 - far) & 7) * 8 + (r32 & 7)
        halves.append(dot_nt((e32 == origin).astype(F32).astype(BF), both))
    for q in range(3):
        lanes = iota((32, 128), 1)
        base = (lax.div(lanes, 16) & 3) * 128
        t_tile = jnp.concatenate([halves[0][:, q * 64 : q * 64 + 64], halves[1][:, q * 64 : q * 64 + 64]], axis=1)
        w_tile = jnp.concatenate(
            [halves[0][:, 192 + q * 64 : 256 + q * 64], halves[1][:, 192 + q * 64 : 256 + q * 64]], axis=1
        )
        rows_t[q] = t_tile.astype(I32) + base
        rows_w[q] = w_tile

    def build(b):
        @pl.loop(0, 8)
        def _(i):
            r = b * 8 + i
            for q in range(3):
                t = rows_t[q, pl.ds(r, 1), :]
                w = rows_w[q, pl.ds(r, 1), :]
                scat[q, :, pl.ds(pl.multiple_of(r * 128, 128), 128)] = jnp.where(
                    iota((512, 128), 0) == t, w, 0.0
                ).astype(BF)

    def scatter_part(b, q):
        rows = jnp.concatenate([in1[b, i, :, q * 128 : q * 128 + 128] for i in range(NX)], axis=1)
        acc[:, q * 512 : q * 512 + 512] += dot_nt(rows, scat[q, :, b * 1024 : b * 1024 + 1024])

    def arrive_batch(b):
        for k in range(1, NX):
            for half in range(2):
                arrived(in1.at[b, mod(xc + NX - k, NX), pl.ds(half * 32, 32)], xrecv.at[b * 2 + half, k])

    def scatter(b):
        arrive_batch(b)
        for q in range(3):
            scatter_part(b, q)

    def multiply(low, high):
        @pl.loop(low, high)
        def _(r):
            for i in range(6):
                t = r * 6 + i
                cols = jnp.zeros((80, 128), BF)
                for q in range(NF):
                    cols = jnp.where(ids[1, t] == q, ftd[:, q * 128 : q * 128 + 128], cols)
                prod[t] = dot_nt(cols, tiles[t])

    build(0)
    build(1)
    in1[:, :, COLS:80, :] = jnp.ones((4, NX, 16, 384), BF)
    z[CPAD:256] = jnp.zeros((256 - CPAD, NODES), BF)
    ftd[0:COLS] = feat[...]
    ftd[COLS:80] = jnp.ones((16, NODES), BF)

    took(1, 0)
    pass_on(1, 2, 0, up)
    took(7, 0)
    pass_on(7, 6, 0, down)
    arrived(idx_in.at[1], irecv.at[1])
    gather(1, 0)
    merge_and_send(0, 0)
    took(1, 1)
    pass_on(1, 2, 1, up)
    took(7, 1)
    pass_on(7, 6, 1, down)
    gather(1, 1)
    merge_and_send(0, 1)
    arrived(idx_in.at[7], irecv.at[7])
    gather(7, 0)
    loads[5].wait()
    multiply(0, 3)

    took(2, 0)
    pass_on(2, 3, 0, up)
    took(6, 0)
    pass_on(6, 5, 0, down)
    arrived(idx_in.at[2], irecv.at[2])
    gather(2, 0)
    merge_and_send(1, 0)
    gather(7, 1)
    took(2, 1)
    pass_on(2, 3, 1, up)
    took(6, 1)
    pass_on(6, 5, 1, down)
    gather(2, 1)
    merge_and_send(1, 1)
    build(2)
    arrived(idx_in.at[6], irecv.at[6])
    gather(6, 0)

    took(3, 0)
    pass_on(3, 4, 0, up)
    took(5, 0)
    arrived(idx_in.at[3], irecv.at[3])
    gather(3, 0)
    merge_and_send(2, 0)
    gather(6, 1)
    took(3, 1)
    took(5, 1)
    pass_on(5, 4, 1, down)
    gather(3, 1)
    merge_and_send(2, 1)
    arrived(idx_in.at[5], irecv.at[5])
    gather(5, 0)
    gather(5, 1)
    build(3)
    multiply(3, 6)
    took(4, 0)
    arrived(idx_in.at[4], irecv.at[4])
    gather(4, 0)
    took(4, 1)
    gather(4, 1)
    for q in range(3):
        last_batch(q)

    @pl.loop(0, NF)
    def _(p):
        r = mod(p, 4) * 3 + lax.div(p, 4)
        total = jnp.zeros((80, 128), F32)
        for t in range(36):
            total = total + jnp.where(ids[0, t] == r, prod[t], 0.0)
        acc[:, pl.ds(pl.multiple_of(p * 128, 128), 128)] = total

    scatter(0)
    scatter(1)
    scatter(2)
    loads[6].wait()
    for k in range(1, NF):
        arrived(frows.at[mod(f + NF - k, NF)], frecv.at[k])
    pre[...] = dot(frows[...].reshape(768, 128).T, s1[...])
    for q in range(3):
        for k in range(1, NX):
            arrived(in1.at[3, mod(xc + NX - k, NX), pl.ds(0, COLS), pl.ds(q * 128, 128)], xrecv.at[6 + q, k])
        scatter_part(3, q)
        for i in range(4):
            place = mod(lax.div(f, 3) + i, 4)
            g = place * 3 + q
            part = acc[:, pl.ds(pl.multiple_of(q * 512 + place * 128, 128), 128)]
            nsend_buf[g] = (part[0:COLS] / part[COLS : COLS + 1]).astype(BF)

            @pl.when(f != g)
            def _():
                remote(nsend_buf.at[g], nrows.at[f], nsend.at[g], nrecv.at[f], g, d).start()

    nrows[f] = nsend_buf[f]
    deg[...] = acc[COLS : COLS + 8, pl.ds(pl.multiple_of(mod(f, 3) * 512 + lax.div(f, 3) * 128, 128), 128)]
    loads[7].wait()
    loads[8].wait()
    wno[CLS - 9 : CPAD] = jnp.zeros((16, HID), BF)
    wno[0:CLS] = no[...]
    s2 = sources[f]
    high2 = (s2 >> 8).astype(F32).astype(BF)
    low2 = (s2 & 255).astype(F32).astype(BF)

    @pl.loop(0, 8)
    def _(j):
        rows = iota((128, ND), 0) + j * 128
        expand = (lax.div(rows, 16) == iota((128, ND), 1)).astype(F32).astype(BF)
        value = dot_nt(expand, high2) * 256.0 + dot_nt(expand, low2)
        mine = (iota((128, 16), 0) & 15) == iota((128, 16), 1)
        node = jnp.sum(jnp.where(mine, value, 0.0), axis=1, keepdims=True).astype(I32)
        for q in range(NF):
            oh2[pl.ds(pl.multiple_of(j * 128, 128), 128), q * 128 : q * 128 + 128] = (
                (iota((128, 128), 1) + q * 128) == node
            ).astype(F32).astype(BF)

    for k in range(1, NF):
        g = mod(f + NF - k, NF)
        arrived(nrows.at[g], nrecv.at[g])

    hidden = jnp.maximum(pre[...] + dot(nrows[...].reshape(768, 128).T, n1[...]), 0.0).astype(BF)
    hidden_ref[...] = hidden

    def block_at(g):
        return z.at[pl.ds(0, CPAD), pl.ds(pl.multiple_of(g * 128, 128), 128)]

    z[0:CPAD, pl.ds(pl.multiple_of(f * 128, 128), 128)] = dot_nt(wno[...], hidden_ref[...]).astype(BF)

    way = 1 - 2 * core
    ways = (way, -way)

    def from_far(side, k):
        return block_at(mod(f + NF - ways[side] * k, NF))

    def throw(side, held, hops):
        block = from_far(side, held)
        k = held + hops
        go(remote(block, block, zsend.at[side, k], zrecv.at[side, k], mod(f + NF + ways[side] * hops, NF), d))

    def caught(side, k):
        arrived(from_far(side, k), zrecv.at[side, k])

    for hops in (4, 2, 1):
        for side in range(2):
            throw(side, 0, hops)
    caught(0, 4)
    throw(0, 4, 2)
    throw(0, 4, 1)
    caught(1, 4)
    throw(1, 4, 1)
    for side in range(2):
        caught(side, 2)
        throw(side, 2, 1)

    loads[9].wait()
    wso[CLS - 9 : CPAD] = jnp.zeros((16, HID), BF)
    wso[0:CLS] = so[...]
    own_term = dot_nt(wso[...], hidden_ref[...])
    lane = iota((ND, 1024), 1)
    spread = (lax.div(lane, 16) == iota((ND, 1024), 0)).astype(F32).astype(BF)
    t2 = jnp.where(iota((16, ND), 0) < counts[f], targets[f], -512).astype(F32).astype(BF)
    own = iota((16, 1024), 0) == (iota((16, 1024), 1) & 15)
    t_row = jnp.sum(jnp.where(own, dot(t2, spread), 0.0), axis=0, keepdims=True).astype(I32)
    w_row = jnp.sum(jnp.where(own, dot(weights[f], spread), 0.0), axis=0, keepdims=True)
    scat2[...] = jnp.where(iota((128, 1024), 0) == t_row, w_row, 0.0).astype(BF)

    @pl.loop(0, NF)
    def _(q):
        block = jnp.zeros((128, 128), BF)
        for t in range(36):
            block = jnp.where((ids[0, t] == f) & (ids[1, t] == q), tiles[t], block)
        band[:, pl.ds(pl.multiple_of(q * 128, 128), 128)] = block

    for k in (1, 3, 5):
        caught(0, k)
        caught(1, k)
    caught(0, 6)

    def quarter(j):
        base = mod(lax.div(d, 16) + j, 4) * 16
        rows = pl.ds(pl.multiple_of(base * 16, 256), 256)
        got = dot_nt(oh2[rows], z[...])
        out2[rows] = got[:, 0:128].astype(BF)
        rest = got[:, 128:160]
        for half in range(2):
            outb[lax.div(base, 8) + half] = jnp.concatenate(
                [rest[(half * 8 + i) * 16 : (half * 8 + i) * 16 + 16] for i in range(NX)], axis=1
            ).astype(BF)

    def straight(j):
        base = mod(lax.div(d, 16) + j, 4) * 16

        @pl.loop(0, 16)
        def _(k):
            to = base + mod(d + k, 16)

            @pl.when(to != d)
            def _():
                remote(
                    out2.at[pl.ds(pl.multiple_of(to * 16, 16), 16)], in2.at[pl.ds(pl.multiple_of(d * 16, 16), 16)],
                    asend, arecv, f, to,
                ).start()

    for j in range(4):
        quarter(j)
    for k in range(1, NY):
        to = mod(y + k, NY)
        go(remote(outb.at[to], inb.at[y], bsend.at[0, k], brecv.at[0, k], f, to * NX + xc))
    inb[y] = outb[y]
    straight(2)
    straight(1)

    for k in range(1, NY):
        arrived(inb.at[mod(y + NY - k, NY)], brecv.at[0, k])
    for i in range(NX):
        outb2[i] = jnp.concatenate(
            [inb[r, :, i * 32 : i * 32 + 32].astype(F32) for r in range(NY)], axis=1
        ).astype(BF)
    for k in range(1, NX):
        to = mod(xc + k, NX)
        go(remote(outb2.at[to], inb2.at[xc], bsend.at[1, k], brecv.at[1, k], f, y * NX + to))
    inb2[xc] = outb2[xc]
    straight(3)
    straight(0)
    mine = pl.ds(pl.multiple_of(d * 16, 16), 16)
    in2[mine] = out2[mine]
    total = dot_nt(band[...], z[...])


    for k in range(1, NX):
        arrived(inb2.at[mod(xc + NX - k, NX)], brecv.at[1, k])
    flat = inb2[...].reshape(128, 256).astype(F32)
    flat = jnp.concatenate([flat[:, r * 32 : r * 32 + 32] for r in range(NY)], axis=0).astype(BF)
    few = dot(scat2[...], flat)
    total_b = total[:, 128:256] + jnp.concatenate([few, jnp.zeros((128, 96), F32)], axis=1)
    logits_ref[128:CLS, 0, :] = own_term[128:CLS] + (total_b.T)[0 : CLS - 128] / deg[0:1]

    arrived(in2.at[pl.ds(0, 1008)], arecv)
    total_a = total[:, 0:128] + dot(scat2[...], in2[...])
    logits_ref[0:128, 0, :] = own_term[0:128] + total_a.T / deg[0:1]

    arrived(out2.at[pl.ds(0, 1008)], asend)
    for k in range(1, NF):
        g = mod(f + k, NF)
        arrived(nsend_buf.at[g], nsend.at[g])
    for copy in sent:
        copy.wait_send()


def hand_over(hidden_ref, logits_ref, hidden_out, logits_out):
    hidden_out[...] = hidden_ref[...]
    logits_out[...] = logits_ref[...]


def on_device(
    features, tiles, tile_ids, sources, targets, counts, edge_weight, self_one, neigh_one, self_out, neigh_out
):
    vmem = pl.BlockSpec(memory_space=pltpu.VMEM)
    anywhere = pl.BlockSpec(memory_space=pl.ANY)
    dma = pltpu.SemaphoreType.DMA
    hidden, logits = pl.pallas_call(
        kernel,
        out_shape=(jax.ShapeDtypeStruct((128, HID), BF), jax.ShapeDtypeStruct((CLS, 1, 128), F32)),
        in_specs=[pl.BlockSpec(memory_space=pltpu.SMEM)] + [anywhere] * 10,
        out_specs=(vmem, vmem),
        scratch_shapes=[
            pltpu.VMEM((NF, 1, ND), I32),
            pltpu.VMEM((NF, 16, ND), I32),
            pltpu.VMEM((NF, 16, ND), I32),
            pltpu.VMEM((NF, 16, ND), BF),
            pltpu.VMEM((COLS, NODES), BF),
            pltpu.VMEM((CLS, HID), BF),
            pltpu.VMEM((CLS, HID), BF),
            pltpu.VMEM((36, 128, 128), BF),
            pltpu.VMEM((768, HID), BF),
            pltpu.VMEM((768, HID), BF),
            pltpu.VMEM((NY, COLS, NODES), BF),
            pltpu.VMEM((NY, 16, 128), I16),
            pltpu.VMEM((NY, 16, 128), I16),
            pltpu.VMEM((NY, COLS, NODES), BF),
            pltpu.VMEM((4, NX, COLS, 384), BF),
            pltpu.VMEM((4, NX, 80, 384), BF),
            pltpu.VMEM((80, NODES), BF),
            pltpu.VMEM((3, 512, 4096), BF),
            pltpu.VMEM((3, 32, 128), I32),
            pltpu.VMEM((3, 32, 128), F32),
            pltpu.VMEM((80, NODES), F32),
            pltpu.VMEM((NF, COLS, 128), BF),
            pltpu.VMEM((NF, COLS, 128), BF),
            pltpu.VMEM((NF, COLS, 128), BF),
            pltpu.VMEM((128, HID), F32),
            pltpu.VMEM((CPAD, HID), BF),
            pltpu.VMEM((CPAD, HID), BF),
            pltpu.VMEM((256, NODES), BF),
            pltpu.VMEM((1024, NODES), BF),
            pltpu.VMEM((128, 1024), BF),
            pltpu.VMEM((1024, 128), BF),
            pltpu.VMEM((1024, 128), BF),
            pltpu.VMEM((8, 128), F32),
            pltpu.VMEM((36, 80, 128), F32),
            pltpu.VMEM((128, NODES), BF),
            pltpu.VMEM((NY, 16, 256), BF),
            pltpu.VMEM((NY, 16, 256), BF),
            pltpu.VMEM((NY, 16, 256), BF),
            pltpu.VMEM((NY, 16, 256), BF),
            dma((10,)),
            dma((NY, 2)), dma((NY, 2)),
            dma((NY,)), dma((NY,)),
            dma((NF,)), dma((NF,)),
            dma((9, NX)), dma((9, NX)),
            dma((NF,)), dma((NF,)),
            dma((2, 7)), dma((2, 7)),
            dma, dma,
            dma((2, 8)), dma((2, 8)),
        ],
        compiler_params=pltpu.CompilerParams(
            collective_id=0, has_side_effects=True, vmem_limit_bytes=56 * 1024 * 1024
        ),
    )(
        tile_ids[0].T,
        jnp.transpose(counts, (2, 0, 1)),
        jnp.transpose(sources[0], (1, 2, 0)),
        jnp.transpose(targets[0], (1, 2, 0)),
        jnp.transpose(edge_weight[0], (1, 2, 0)),
        features[0].T,
        tiles[0],
        self_one,
        neigh_one,
        self_out.T,
        neigh_out.T,
    )
    hidden, logits = pl.pallas_call(
        hand_over,
        out_shape=(jax.ShapeDtypeStruct((128, HID), BF), jax.ShapeDtypeStruct((CLS, 1, 128), F32)),
        in_specs=[vmem] * 2,
        out_specs=(vmem, vmem),
    )(hidden, logits)
    return hidden[None], jnp.transpose(logits, (1, 0, 2))


def solution(mesh):
    placed = (
        P("dom", None, "feat"),
        P("dom", None, None, None),
        P("dom", None, None),
        P("dom", None, None, None),
        P("dom", None, None, None),
        P("dom", None, None),
        P("dom", None, None, None),
        P(),
        P(),
        P(),
        P(),
    )
    return jax.shard_map(
        on_device,
        mesh=mesh,
        in_specs=placed,
        out_specs=(P("dom", "feat", None), P("dom", None, "feat")),
        check_vma=False,
    )
```

```python
import jax
import jax.numpy as jnp
from jax import lax
from jax.experimental import pallas as pl
from jax.experimental.pallas import tpu as pltpu
from jax.sharding import PartitionSpec as P

MESH = pl.DeviceIdType.MESH
BF = jnp.bfloat16
F32 = jnp.float32
I32 = jnp.int32
I16 = jnp.int16
NT = (((1,), (1,)), ((), ()))

NF = 12
ND = 64
NY = 8
NX = 8
COLS = 64
NODES = 1536
HID = 1024
CLS = 153
CPAD = 160
PAIRS = ((0, 1), (2, 7), (6, 3), (4, 5))


def iota(shape, dim):
    return lax.broadcasted_iota(I32, shape, dim)


def mod(a, n):
    return lax.rem(a, jnp.int32(n))


def dot(a, b):
    return jnp.dot(a, b, preferred_element_type=F32)


def dot_nt(a, b):
    return lax.dot_general(a, b, NT, preferred_element_type=F32)


def kernel(
    ids, counts_hbm, sources_hbm, targets_hbm, weights_hbm, feat_hbm, tiles_hbm, s1_hbm, n1_hbm, so_hbm, no_hbm,
    hidden_ref, logits_ref,
    counts, sources, targets, weights, feat, so, no, tiles, s1, n1, tab, idx_out, idx_in, picked, out1, in1, ftd, scat, rows_t, rows_w, acc,
    frows, nsend_buf, nrows, pre, wso, wno, z, oh2, scat2, out2, in2, deg, prod, band, outb, inb, outb2, inb2,
    loc, tsend, trecv, isend, irecv, fsend, frecv, xsend, xrecv, nsend, nrecv, zsend, zrecv, asend, arecv, bsend, brecv,
):
    f = lax.axis_index("feat")
    d = lax.axis_index("dom")
    y = lax.div(d, jnp.int32(NX))
    xc = mod(d, NX)
    core = mod(d, 2)

    def remote(src, dst, ss, rs, fi, di):
        return pltpu.make_async_remote_copy(
            src_ref=src, dst_ref=dst, send_sem=ss, recv_sem=rs, device_id=(fi, di), device_id_type=MESH
        )

    def arrived(dst, rs):
        pltpu.make_async_copy(dst, dst, rs).wait()

    def row_peer(k):
        return mod(y + k, NY) * NX + xc

    def col_peer(k):
        return y * NX + mod(xc + k, NX)

    barrier = pltpu.get_barrier_semaphore()
    for k in range(1, NY):
        pl.semaphore_signal(barrier, inc=1, device_id=(f, row_peer(k)), device_id_type=MESH)
    for k in range(1, NX):
        pl.semaphore_signal(barrier, inc=1, device_id=(f, col_peer(k)), device_id_type=MESH)
    for k in range(1, NF):
        pl.semaphore_signal(barrier, inc=1, device_id=(mod(f + k, NF), d), device_id_type=MESH)

    loads = [
        pltpu.make_async_copy(far, near, loc.at[i])
        for i, (far, near) in enumerate((
            (sources_hbm, sources), (feat_hbm, feat), (targets_hbm, targets), (counts_hbm, counts),
            (weights_hbm, weights), (tiles_hbm, tiles), (s1_hbm, s1), (n1_hbm, n1), (no_hbm, no), (so_hbm, so),
        ))
    ]
    for load in loads:
        load.start()

    pl.semaphore_wait(barrier, NY - 1 + NX - 1 + NF - 1)

    sent = []

    def go(copy):
        copy.start()
        sent.append(copy)

    def table(slot):
        return feat if slot == 0 else tab.at[slot]

    def travels(slot):
        return feat_hbm if slot == 0 else tab.at[slot]

    def pass_on(from_slot, to_slot, half, di):
        part = pl.ds(half * 32, 32)
        go(remote(
            travels(from_slot).at[part], tab.at[to_slot, part],
            tsend.at[to_slot, half], trecv.at[to_slot, half], f, di,
        ))

    def took(slot, half):
        arrived(tab.at[slot, pl.ds(half * 32, 32)], trecv.at[slot, half])

    up = row_peer(1)
    down = row_peer(NY - 1)
    for half in range(2):
        pass_on(0, 1, half, up)
        pass_on(0, 7, half, down)
    spread_out = [place * 3 + third for third in range(3) for place in range(4)]

    loads[0].wait()
    src = jnp.concatenate([sources[g] for g in spread_out], axis=0)
    both = jnp.concatenate([src >> 8, src & 255], axis=0).astype(F32).astype(BF)
    r32 = iota((32, ND), 0)
    e32 = iota((32, ND), 1)
    flip = (lax.div(r32, 4) + y) & 1
    halves = []
    for h in range(2):
        pick = (e32 == r32 * 2 + (flip ^ h)).astype(F32).astype(BF)
        got = dot_nt(pick, both)
        halves.append((got[:, :192] * 256.0 + got[:, 192:]).astype(I32))
    thirds = [
        jnp.concatenate([halves[0][:, q * 64 : q * 64 + 64], halves[1][:, q * 64 : q * 64 + 64]], axis=1)
        for q in range(3)
    ]
    for row in range(NY):
        some = [third[row * 4 : row * 4 + 4] for third in thirds] + [jnp.zeros((4, 128), I32)]
        idx_out[row] = jnp.concatenate(some, axis=0).astype(I16)
    idx_in[0] = idx_out[y]


    for k in range(1, NY):
        to = mod(y + k, NY)
        go(remote(idx_out.at[to], idx_in.at[k], isend.at[k], irecv.at[k], f, to * NX + xc))
    for k in range(1, NF):
        g = mod(f + k, NF)
        go(remote(
            feat_hbm.at[:, pl.ds(pl.multiple_of(g * 128, 128), 128)], frows.at[f], fsend.at[k], frecv.at[k], g, d
        ))
    loads[1].wait()
    frows[f] = feat[:, pl.ds(pl.multiple_of(f * 128, 128), 128)]

    def gather(slot, half):
        here = table(slot)
        rows = slice(half * 32, half * 32 + 32)
        ids_here = idx_in[slot].astype(I32)
        for r in range(6):
            wide = jnp.concatenate([here[rows, k * 256 : k * 256 + 256] for k in range(6)], axis=0)
            pick = jnp.concatenate([ids_here[2 * r : 2 * r + 1], ids_here[2 * r + 1 : 2 * r + 2]], axis=1)
            low = pick & 255
            high = pick >> 8
            one_hot = (iota((256, 256), 0) == low).astype(F32).astype(BF)
            got = dot(wide, one_hot)
            kept = jnp.zeros((32, 256), F32)
            for k in range(6):
                kept = jnp.where(high == k, got[k * 32 : k * 32 + 32], kept)
            picked[slot, rows, r * 256 : r * 256 + 256] = kept.astype(BF)

    first_half = iota((COLS, 128), 1) < 64

    def merge(b, q):
        even, odd = PAIRS[b]
        for col in range(4):
            at = (q * 4 + col) * 128
            one = picked[even, :, at : at + 128]
            two = picked[odd, :, at : at + 128]
            out1[b, 2 * col, :, q * 128 : q * 128 + 128] = jnp.where(first_half, one, two)
            out1[b, 2 * col + 1, :, q * 128 : q * 128 + 128] = jnp.where(first_half, two, one)

    def merge_and_send(b, half):
        even, odd = PAIRS[b]
        rows = slice(half * 32, half * 32 + 32)
        for q in range(3):
            for col in range(4):
                at = (q * 4 + col) * 128
                one = picked[even, rows, at : at + 128]
                two = picked[odd, rows, at : at + 128]
                out1[b, 2 * col, rows, q * 128 : q * 128 + 128] = jnp.where(first_half[rows], one, two)
                out1[b, 2 * col + 1, rows, q * 128 : q * 128 + 128] = jnp.where(first_half[rows], two, one)
        part = pl.ds(half * 32, 32)
        for k in (4, 3, 5, 2, 6, 1, 7):
            to = mod(xc + k, NX)
            go(remote(
                out1.at[b, to, part], in1.at[b, xc, part],
                xsend.at[b * 2 + half, k], xrecv.at[b * 2 + half, k], f, y * NX + to,
            ))
        in1[b, xc, rows] = out1[b, xc, rows]

    def last_batch(q):
        merge(3, q)
        part = pl.ds(q * 128, 128)
        for k in (4, 3, 5, 2, 6, 1, 7):
            to = mod(xc + k, NX)
            go(remote(
                out1.at[3, to, :, part], in1.at[3, xc, pl.ds(0, COLS), part],
                xsend.at[6 + q, k], xrecv.at[6 + q, k], f, y * NX + to,
            ))
        in1[3, xc, 0:COLS, part] = out1[3, xc, :, part]

    gather(0, 0)
    gather(0, 1)

    for i in (2, 3, 4):
        loads[i].wait()
    t_all = jnp.concatenate(
        [jnp.where(iota((16, ND), 0) < counts[g], targets[g], -512) for g in spread_out], axis=0
    )
    w_all = jnp.concatenate([weights[g] for g in spread_out], axis=0)
    both = jnp.concatenate([t_all.astype(F32).astype(BF), w_all], axis=0)
    batch = lax.div(r32, 8)
    halves = []
    for h in range(2):
        par = core ^ h
        far = jnp.zeros((32, ND), I32)
        for b in range(4):
            dist = jnp.where(par == 0, PAIRS[b][0], PAIRS[b][1])
            far = jnp.where(batch == b, dist, far)
        origin = ((y + 8 - far) & 7) * 8 + (r32 & 7)
        halves.append(dot_nt((e32 == origin).astype(F32).astype(BF), both))
    for q in range(3):
        lanes = iota((32, 128), 1)
        base = (lax.div(lanes, 16) & 3) * 128
        t_tile = jnp.concatenate([halves[0][:, q * 64 : q * 64 + 64], halves[1][:, q * 64 : q * 64 + 64]], axis=1)
        w_tile = jnp.concatenate(
            [halves[0][:, 192 + q * 64 : 256 + q * 64], halves[1][:, 192 + q * 64 : 256 + q * 64]], axis=1
        )
        rows_t[q] = t_tile.astype(I32) + base
        rows_w[q] = w_tile

    def build(b):
        @pl.loop(0, 8)
        def _(i):
            r = b * 8 + i
            for q in range(3):
                t = rows_t[q, pl.ds(r, 1), :]
                w = rows_w[q, pl.ds(r, 1), :]
                scat[q, :, pl.ds(pl.multiple_of(r * 128, 128), 128)] = jnp.where(
                    iota((512, 128), 0) == t, w, 0.0
                ).astype(BF)

    def scatter_part(b, q):
        rows = jnp.concatenate([in1[b, i, :, q * 128 : q * 128 + 128] for i in range(NX)], axis=1)
        acc[:, q * 512 : q * 512 + 512] += dot_nt(rows, scat[q, :, b * 1024 : b * 1024 + 1024])

    def arrive_batch(b):
        for k in range(1, NX):
            for half in range(2):
                arrived(in1.at[b, mod(xc + NX - k, NX), pl.ds(half * 32, 32)], xrecv.at[b * 2 + half, k])

    def scatter(b):
        arrive_batch(b)
        for q in range(3):
            scatter_part(b, q)

    def multiply(low, high):
        @pl.loop(low, high)
        def _(r):
            for i in range(6):
                t = r * 6 + i
                cols = jnp.zeros((80, 128), BF)
                for q in range(NF):
                    cols = jnp.where(ids[1, t] == q, ftd[:, q * 128 : q * 128 + 128], cols)
                prod[t] = dot_nt(cols, tiles[t])

    build(0)
    build(1)
    in1[:, :, COLS:80, :] = jnp.ones((4, NX, 16, 384), BF)
    z[CPAD:256] = jnp.zeros((256 - CPAD, NODES), BF)
    ftd[0:COLS] = feat[...]
    ftd[COLS:80] = jnp.ones((16, NODES), BF)

    took(1, 0)
    pass_on(1, 2, 0, up)
    took(7, 0)
    pass_on(7, 6, 0, down)
    arrived(idx_in.at[1], irecv.at[1])
    gather(1, 0)
    merge_and_send(0, 0)
    took(1, 1)
    pass_on(1, 2, 1, up)
    took(7, 1)
    pass_on(7, 6, 1, down)
    gather(1, 1)
    merge_and_send(0, 1)
    arrived(idx_in.at[7], irecv.at[7])
    gather(7, 0)
    loads[5].wait()
    multiply(0, 3)

    took(2, 0)
    pass_on(2, 3, 0, up)
    took(6, 0)
    pass_on(6, 5, 0, down)
    arrived(idx_in.at[2], irecv.at[2])
    gather(2, 0)
    merge_and_send(1, 0)
    gather(7, 1)
    took(2, 1)
    pass_on(2, 3, 1, up)
    took(6, 1)
    pass_on(6, 5, 1, down)
    gather(2, 1)
    merge_and_send(1, 1)
    build(2)
    arrived(idx_in.at[6], irecv.at[6])
    gather(6, 0)

    took(3, 0)
    pass_on(3, 4, 0, up)
    took(5, 0)
    arrived(idx_in.at[3], irecv.at[3])
    gather(3, 0)
    merge_and_send(2, 0)
    gather(6, 1)
    took(3, 1)
    took(5, 1)
    pass_on(5, 4, 1, down)
    gather(3, 1)
    merge_and_send(2, 1)
    arrived(idx_in.at[5], irecv.at[5])
    gather(5, 0)
    gather(5, 1)
    build(3)
    multiply(3, 6)
    took(4, 0)
    arrived(idx_in.at[4], irecv.at[4])
    gather(4, 0)
    took(4, 1)
    gather(4, 1)
    for q in range(3):
        last_batch(q)

    @pl.loop(0, NF)
    def _(p):
        r = mod(p, 4) * 3 + lax.div(p, 4)
        total = jnp.zeros((80, 128), F32)
        for t in range(36):
            total = total + jnp.where(ids[0, t] == r, prod[t], 0.0)
        acc[:, pl.ds(pl.multiple_of(p * 128, 128), 128)] = total

    scatter(0)
    scatter(1)
    scatter(2)
    loads[6].wait()
    for k in range(1, NF):
        arrived(frows.at[mod(f + NF - k, NF)], frecv.at[k])
    pre[...] = dot(frows[...].reshape(768, 128).T, s1[...])
    for q in range(3):
        for k in range(1, NX):
            arrived(in1.at[3, mod(xc + NX - k, NX), pl.ds(0, COLS), pl.ds(q * 128, 128)], xrecv.at[6 + q, k])
        scatter_part(3, q)
        for i in range(4):
            place = mod(lax.div(f, 3) + i, 4)
            g = place * 3 + q
            part = acc[:, pl.ds(pl.multiple_of(q * 512 + place * 128, 128), 128)]
            nsend_buf[g] = (part[0:COLS] / part[COLS : COLS + 1]).astype(BF)

            @pl.when(f != g)
            def _():
                remote(nsend_buf.at[g], nrows.at[f], nsend.at[g], nrecv.at[f], g, d).start()

    nrows[f] = nsend_buf[f]
    deg[...] = acc[COLS : COLS + 8, pl.ds(pl.multiple_of(mod(f, 3) * 512 + lax.div(f, 3) * 128, 128), 128)]
    loads[7].wait()
    loads[8].wait()
    wno[CLS - 9 : CPAD] = jnp.zeros((16, HID), BF)
    wno[0:CLS] = no[...]
    s2 = sources[f]
    high2 = (s2 >> 8).astype(F32).astype(BF)
    low2 = (s2 & 255).astype(F32).astype(BF)

    @pl.loop(0, 8)
    def _(j):
        rows = iota((128, ND), 0) + j * 128
        expand = (lax.div(rows, 16) == iota((128, ND), 1)).astype(F32).astype(BF)
        value = dot_nt(expand, high2) * 256.0 + dot_nt(expand, low2)
        mine = (iota((128, 16), 0) & 15) == iota((128, 16), 1)
        node = jnp.sum(jnp.where(mine, value, 0.0), axis=1, keepdims=True).astype(I32)
        for q in range(NF):
            oh2[pl.ds(pl.multiple_of(j * 128, 128), 128), q * 128 : q * 128 + 128] = (
                (iota((128, 128), 1) + q * 128) == node
            ).astype(F32).astype(BF)

    for k in range(1, NF):
        g = mod(f + NF - k, NF)
        arrived(nrows.at[g], nrecv.at[g])

    hidden = jnp.maximum(pre[...] + dot(nrows[...].reshape(768, 128).T, n1[...]), 0.0).astype(BF)
    hidden_ref[...] = hidden

    def block_at(g):
        return z.at[pl.ds(0, CPAD), pl.ds(pl.multiple_of(g * 128, 128), 128)]

    z[0:CPAD, pl.ds(pl.multiple_of(f * 128, 128), 128)] = dot_nt(wno[...], hidden_ref[...]).astype(BF)

    way = 1 - 2 * core
    ways = (way, -way)

    def from_far(side, k):
        return block_at(mod(f + NF - ways[side] * k, NF))

    def throw(side, held, hops):
        block = from_far(side, held)
        k = held + hops
        go(remote(block, block, zsend.at[side, k], zrecv.at[side, k], mod(f + NF + ways[side] * hops, NF), d))

    def caught(side, k):
        arrived(from_far(side, k), zrecv.at[side, k])

    for hops in (4, 2, 1):
        for side in range(2):
            throw(side, 0, hops)
    caught(0, 4)
    throw(0, 4, 2)
    throw(0, 4, 1)
    caught(1, 4)
    throw(1, 4, 1)
    for side in range(2):
        caught(side, 2)
        throw(side, 2, 1)

    loads[9].wait()
    wso[CLS - 9 : CPAD] = jnp.zeros((16, HID), BF)
    wso[0:CLS] = so[...]
    own_term = dot_nt(wso[...], hidden_ref[...])
    lane = iota((ND, 1024), 1)
    spread = (lax.div(lane, 16) == iota((ND, 1024), 0)).astype(F32).astype(BF)
    t2 = jnp.where(iota((16, ND), 0) < counts[f], targets[f], -512).astype(F32).astype(BF)
    own = iota((16, 1024), 0) == (iota((16, 1024), 1) & 15)
    t_row = jnp.sum(jnp.where(own, dot(t2, spread), 0.0), axis=0, keepdims=True).astype(I32)
    w_row = jnp.sum(jnp.where(own, dot(weights[f], spread), 0.0), axis=0, keepdims=True)
    scat2[...] = jnp.where(iota((128, 1024), 0) == t_row, w_row, 0.0).astype(BF)

    @pl.loop(0, NF)
    def _(q):
        block = jnp.zeros((128, 128), BF)
        for t in range(36):
            block = jnp.where((ids[0, t] == f) & (ids[1, t] == q), tiles[t], block)
        band[:, pl.ds(pl.multiple_of(q * 128, 128), 128)] = block

    for k in (1, 3, 5):
        caught(0, k)
        caught(1, k)
    caught(0, 6)

    def quarter(j):
        base = mod(lax.div(d, 16) + j, 4) * 16
        rows = pl.ds(pl.multiple_of(base * 16, 256), 256)
        got = dot_nt(oh2[rows], z[...])
        out2[rows] = got[:, 0:128].astype(BF)
        rest = got[:, 128:160]
        for half in range(2):
            outb[lax.div(base, 8) + half] = jnp.concatenate(
                [rest[(half * 8 + i) * 16 : (half * 8 + i) * 16 + 16] for i in range(NX)], axis=1
            ).astype(BF)

    def straight(j):
        base = mod(lax.div(d, 16) + j, 4) * 16

        @pl.loop(0, 16)
        def _(k):
            to = base + mod(d + k, 16)

            @pl.when(to != d)
            def _():
                remote(
                    out2.at[pl.ds(pl.multiple_of(to * 16, 16), 16)], in2.at[pl.ds(pl.multiple_of(d * 16, 16), 16)],
                    asend, arecv, f, to,
                ).start()

    quarter(2)
    straight(2)
    for j in (0, 1, 3):
        quarter(j)
    for k in range(1, NY):
        to = mod(y + k, NY)
        go(remote(outb.at[to], inb.at[y], bsend.at[0, k], brecv.at[0, k], f, to * NX + xc))
    inb[y] = outb[y]
    for j in (1, 3, 0):
        straight(j)

    mine = pl.ds(pl.multiple_of(d * 16, 16), 16)
    in2[mine] = out2[mine]
    total = dot_nt(band[...], z[...])

    for k in range(1, NY):
        arrived(inb.at[mod(y + NY - k, NY)], brecv.at[0, k])
    for i in range(NX):
        outb2[i] = jnp.concatenate(
            [inb[r, :, i * 32 : i * 32 + 32].astype(F32) for r in range(NY)], axis=1
        ).astype(BF)
    for k in range(1, NX):
        to = mod(xc + k, NX)
        go(remote(outb2.at[to], inb2.at[xc], bsend.at[1, k], brecv.at[1, k], f, y * NX + to))
    inb2[xc] = outb2[xc]
    for k in range(1, NX):
        arrived(inb2.at[mod(xc + NX - k, NX)], brecv.at[1, k])
    flat = inb2[...].reshape(128, 256).astype(F32)
    flat = jnp.concatenate([flat[:, r * 32 : r * 32 + 32] for r in range(NY)], axis=0).astype(BF)
    few = dot(scat2[...], flat)
    total_b = total[:, 128:256] + jnp.concatenate([few, jnp.zeros((128, 96), F32)], axis=1)
    logits_ref[128:CLS, 0, :] = own_term[128:CLS] + (total_b.T)[0 : CLS - 128] / deg[0:1]

    arrived(in2.at[pl.ds(0, 1008)], arecv)
    total_a = total[:, 0:128] + dot(scat2[...], in2[...])
    logits_ref[0:128, 0, :] = own_term[0:128] + total_a.T / deg[0:1]

    arrived(out2.at[pl.ds(0, 1008)], asend)
    for k in range(1, NF):
        g = mod(f + k, NF)
        arrived(nsend_buf.at[g], nsend.at[g])
    for copy in sent:
        copy.wait_send()


def hand_over(hidden_ref, logits_ref, hidden_out, logits_out):
    hidden_out[...] = hidden_ref[...]
    logits_out[...] = logits_ref[...]


def on_device(
    features, tiles, tile_ids, sources, targets, counts, edge_weight, self_one, neigh_one, self_out, neigh_out
):
    vmem = pl.BlockSpec(memory_space=pltpu.VMEM)
    anywhere = pl.BlockSpec(memory_space=pl.ANY)
    dma = pltpu.SemaphoreType.DMA
    hidden, logits = pl.pallas_call(
        kernel,
        out_shape=(jax.ShapeDtypeStruct((128, HID), BF), jax.ShapeDtypeStruct((CLS, 1, 128), F32)),
        in_specs=[pl.BlockSpec(memory_space=pltpu.SMEM)] + [anywhere] * 10,
        out_specs=(vmem, vmem),
        scratch_shapes=[
            pltpu.VMEM((NF, 1, ND), I32),
            pltpu.VMEM((NF, 16, ND), I32),
            pltpu.VMEM((NF, 16, ND), I32),
            pltpu.VMEM((NF, 16, ND), BF),
            pltpu.VMEM((COLS, NODES), BF),
            pltpu.VMEM((CLS, HID), BF),
            pltpu.VMEM((CLS, HID), BF),
            pltpu.VMEM((36, 128, 128), BF),
            pltpu.VMEM((768, HID), BF),
            pltpu.VMEM((768, HID), BF),
            pltpu.VMEM((NY, COLS, NODES), BF),
            pltpu.VMEM((NY, 16, 128), I16),
            pltpu.VMEM((NY, 16, 128), I16),
            pltpu.VMEM((NY, COLS, NODES), BF),
            pltpu.VMEM((4, NX, COLS, 384), BF),
            pltpu.VMEM((4, NX, 80, 384), BF),
            pltpu.VMEM((80, NODES), BF),
            pltpu.VMEM((3, 512, 4096), BF),
            pltpu.VMEM((3, 32, 128), I32),
            pltpu.VMEM((3, 32, 128), F32),
            pltpu.VMEM((80, NODES), F32),
            pltpu.VMEM((NF, COLS, 128), BF),
            pltpu.VMEM((NF, COLS, 128), BF),
            pltpu.VMEM((NF, COLS, 128), BF),
            pltpu.VMEM((128, HID), F32),
            pltpu.VMEM((CPAD, HID), BF),
            pltpu.VMEM((CPAD, HID), BF),
            pltpu.VMEM((256, NODES), BF),
            pltpu.VMEM((1024, NODES), BF),
            pltpu.VMEM((128, 1024), BF),
            pltpu.VMEM((1024, 128), BF),
            pltpu.VMEM((1024, 128), BF),
            pltpu.VMEM((8, 128), F32),
            pltpu.VMEM((36, 80, 128), F32),
            pltpu.VMEM((128, NODES), BF),
            pltpu.VMEM((NY, 16, 256), BF),
            pltpu.VMEM((NY, 16, 256), BF),
            pltpu.VMEM((NY, 16, 256), BF),
            pltpu.VMEM((NY, 16, 256), BF),
            dma((10,)),
            dma((NY, 2)), dma((NY, 2)),
            dma((NY,)), dma((NY,)),
            dma((NF,)), dma((NF,)),
            dma((9, NX)), dma((9, NX)),
            dma((NF,)), dma((NF,)),
            dma((2, 7)), dma((2, 7)),
            dma, dma,
            dma((2, 8)), dma((2, 8)),
        ],
        compiler_params=pltpu.CompilerParams(
            collective_id=0, has_side_effects=True, vmem_limit_bytes=56 * 1024 * 1024
        ),
    )(
        tile_ids[0].T,
        jnp.transpose(counts, (2, 0, 1)),
        jnp.transpose(sources[0], (1, 2, 0)),
        jnp.transpose(targets[0], (1, 2, 0)),
        jnp.transpose(edge_weight[0], (1, 2, 0)),
        features[0].T,
        tiles[0],
        self_one,
        neigh_one,
        self_out.T,
        neigh_out.T,
    )
    hidden, logits = pl.pallas_call(
        hand_over,
        out_shape=(jax.ShapeDtypeStruct((128, HID), BF), jax.ShapeDtypeStruct((CLS, 1, 128), F32)),
        in_specs=[vmem] * 2,
        out_specs=(vmem, vmem),
    )(hidden, logits)
    return hidden[None], jnp.transpose(logits, (1, 0, 2))


def solution(mesh):
    placed = (
        P("dom", None, "feat"),
        P("dom", None, None, None),
        P("dom", None, None),
        P("dom", None, None, None),
        P("dom", None, None, None),
        P("dom", None, None),
        P("dom", None, None, None),
        P(),
        P(),
        P(),
        P(),
    )
    return jax.shard_map(
        on_device,
        mesh=mesh,
        in_specs=placed,
        out_specs=(P("dom", "feat", None), P("dom", None, "feat")),
        check_vma=False,
    )
```
